512 devices in a mesh: dp: 64 (over y, x, core), col: 8 (over z).
Axes of the slice: x: 4, y: 8, z: 8, core: 2. Of those that a mesh axis runs over, the one named last changes fastest.
Arguments:
- gradients: bfloat16 [64, 6, 512, 2048], P('dp', None, None, 'col')
- momentum: float32 [6, 512, 2048], P(None, 'dp', 'col'), may hold values from -48 to 48
- master: float32 [6, 512, 2048], P(None, 'dp', 'col'), may hold values from -0.125 to 0.125
- owners: int32 [6], replicated, may hold values from 0 to 63, as said below
Outputs:
- new_weights: bfloat16 [6, 512, 2048], P(None, None, 'col')
- new_master: float32 [6, 512, 2048], P(None, 'dp', 'col')
- new_momentum: float32 [6, 512, 2048], P(None, 'dp', 'col')
- owned_updates: bfloat16 [64, 2, 512, 2048], P('dp', None, None, 'col')
- owned_rms: float32 [64, 2], P('dp')
The draws below stay inside these ranges and needn't reach their ends.
Inputs may be any that keep to these rules, and one draw needn't show every extreme that they name: `owners`: no owner index appears more than 2 times, and exactly one appears 2 times.
All inputs are finite; a program needn't handle non-finite values.
Results may differ from the reference program's by a relative error of at most 0.04.
Values may be sent and summed in bfloat16 or wider, within the bound.
A program may use at most 64 MiB of HBM per device.

```python
import math
import jax
import jax.numpy as jnp
from jax import lax

KV = 512
D = 2048
NM = 6
NS_STEPS = 3
MOST = 2
N_DP = 64
N_COL = 8


def draw_gradients(key, part):
    key = jax.random.fold_in(key, 11)
    key_base, key_rows, key_cols = jax.random.split(key, 3)
    row_scale = jnp.exp(jax.random.uniform(key_rows, (1, NM, KV, 1), jnp.float32, 0.0, math.log(10.0)))
    col_scale = jnp.exp(jax.random.uniform(key_cols, (1, NM, 1, D), jnp.float32, 0.0, math.log(10.0)))
    replica = 1.0 + 2.0 * jnp.arange(N_DP, dtype=jnp.float32).reshape(N_DP, 1, 1, 1) / max(N_DP - 1, 1)
    position = jnp.arange(D, dtype=jnp.float32).reshape(1, 1, 1, D) / max(D - 1, 1)
    ramp = 1.0 + 2.0 * position
    base = jax.random.normal(key_base, (N_DP, NM, KV, D), jnp.float32)
    return (0.1 * base * row_scale * col_scale * ramp * replica).astype(jnp.bfloat16)


def draw_owners(key, part):
    key = jax.random.fold_in(key, 23)
    key_ids, key_pick, key_order = jax.random.split(key, 3)
    middle = jax.random.permutation(key_ids, N_DP - 2)[:NM - 3].astype(jnp.int32) + 1
    ends = jnp.array([0, N_DP - 1], dtype=jnp.int32)
    distinct = jnp.concatenate([ends, middle])
    which = jax.random.randint(key_pick, (1,), 0, NM - 1)
    extra = jnp.take(distinct, which)
    listed = jnp.concatenate([extra, distinct])
    return jax.random.permutation(key_order, listed).astype(jnp.int32)


def level_of(own_key, extent, cuts, low, top_value):
    def one(axis_at, blocks):
        heights = jax.random.uniform(jax.random.fold_in(jax.random.fold_in(own_key, 6), axis_at), (blocks,), jnp.float32, low / len(cuts), top_value / len(cuts))
        return jnp.repeat(jnp.exp(heights), extent[axis_at] // blocks).reshape((-1,) + (1,) * (len(extent) - axis_at - 1))

    gain = one(*cuts[0])
    for cut in cuts[1:]:
        gain = gain * one(*cut)
    return gain


def bell_draw(own_key, dims, spread, bound, cuts=(), held_as=jnp.bfloat16):
    loudness = level_of(own_key, dims, cuts, -0.22, 0.18) if cuts else 1.0
    values = jax.random.normal(own_key, dims, jnp.float32) * spread * loudness
    return jnp.minimum(jnp.maximum(values, -bound), bound).astype(held_as)


def setup_inputs(seed: int = 0) -> dict:
    seeds = jax.random.split(jax.random.key(seed), 5)
    gradients = draw_gradients(jax.random.fold_in(seeds[4], 71), 0)
    momentum = bell_draw(seeds[1], (NM, KV, D), 8.0, 48.0, ((1, 64), (2, 8)), jnp.float32)
    master = bell_draw(seeds[2], (NM, KV, D), D ** -0.5, 0.125, ((1, 64), (2, 8)), jnp.float32)
    owners = draw_owners(jax.random.fold_in(seeds[4], 71), 0)
    return dict(gradients=gradients, momentum=momentum, master=master, owners=owners)


quintic_first = 3.4445
quintic_second = -4.775
quintic_third = 2.0315
momentum_decay = 0.95
learn_rate = 0.3
weight_decay = 0.1
epsilon = 1e-07

def orthogonalize(update):
    squares = jnp.sum(jnp.square(update.astype(jnp.float32)))
    iterate = (update.astype(jnp.float32) / (jnp.sqrt(squares) + epsilon)).astype(jnp.bfloat16)
    col_width = D // N_COL
    for iteration in range(NS_STEPS):
        blocks = iterate.astype(jnp.float32).reshape(KV, N_COL, col_width)
        partial_value = jnp.einsum('icw,jcw->cij', blocks, blocks)
        rounded = lax.optimization_barrier(partial_value.astype(jnp.bfloat16))
        gram_sum = lax.optimization_barrier(jnp.sum(rounded.astype(jnp.float32), axis=0))
        gram_half = gram_sum.astype(jnp.bfloat16)
        square = jnp.dot(gram_half, gram_half, preferred_element_type=jnp.float32)
        mixing = (quintic_second * gram_sum + quintic_third * square).astype(jnp.bfloat16)
        iterate = (quintic_first * iterate.astype(jnp.float32) + jnp.dot(mixing, iterate, preferred_element_type=jnp.float32)).astype(jnp.bfloat16)
    factor = 0.2 * math.sqrt(max(KV, D))
    return (factor * iterate.astype(jnp.float32)).astype(jnp.bfloat16)

def reference(gradients, momentum, master, owners):

    def accumulate(index, running):
        return running + lax.dynamic_index_in_dim(gradients, index, 0, keepdims=False).astype(jnp.float32)
    summed = lax.fori_loop(0, N_DP, accumulate, jnp.zeros((NM, KV, D), jnp.float32))
    new_momentum = momentum_decay * momentum + summed
    update = (summed + momentum_decay * new_momentum).astype(jnp.bfloat16)
    squares = lax.optimization_barrier(jnp.sum(jnp.square(update.astype(jnp.float32)), axis=(1, 2)))
    matrix_rms = jnp.sqrt(squares / float(KV * D))
    scaled = lax.map(orthogonalize, update)
    new_master = master * (1.0 - learn_rate * weight_decay) - learn_rate * scaled.astype(jnp.float32)
    new_weights = new_master.astype(jnp.bfloat16)
    matches = owners[:, None] == owners[None, :]
    earlier = jnp.arange(NM, dtype=jnp.int32)[None, :] < jnp.arange(NM, dtype=jnp.int32)[:, None]
    slot_index = lax.optimization_barrier(jnp.sum((matches & earlier).astype(jnp.int32), axis=1)).astype(jnp.int32)
    target = owners * MOST + slot_index
    picker = (jnp.arange(N_DP * MOST, dtype=jnp.int32)[:, None] == target[None, :]).astype(jnp.float32)
    owned_updates = jnp.einsum('sm,mkd->skd', picker, scaled.astype(jnp.float32)).astype(jnp.bfloat16)
    owned_updates = owned_updates.reshape(N_DP, MOST, KV, D)
    owned_rms = lax.optimization_barrier(jnp.sum(picker * matrix_rms[None, :], axis=1)).reshape(N_DP, MOST)
    return (new_weights, new_master, new_momentum, owned_updates, owned_rms)
```

```python
import functools
import math

import jax
import jax.numpy as jnp
from jax import lax
from jax.experimental import pallas as pl
from jax.experimental.pallas import tpu as pltpu
from jax.sharding import PartitionSpec as P

KV = 512
D = 2048
NM = 6
MOST = 2
NY = 8
NX = 4
NZ = 8

quintic_first = 3.4445
quintic_second = -4.775
quintic_third = 2.0315
momentum_decay = 0.95
learn_rate = 0.3
weight_decay = 0.1
epsilon = 1e-07
factor = 0.2 * math.sqrt(max(KV, D))

f32 = jnp.float32
bf16 = jnp.bfloat16
HALF = 3

BUFFERS = dict(
    own_g=((NM, KV, 128), bf16),
    sib_g=((NM, KV, 128), bf16),
    sum1=((NX, NM, 128, 128), bf16),
    xr=((NX - 1, NM, 128, 128), bf16),
    sum2=((NM, 128, 128), bf16),
    yr=((NY - 1, 128, 128), bf16),
    mom16=((NM, 16, 128), f32),
    mas16=((NM, 16, 128), f32),
    masb=((NM, 16, 128), bf16),
    momr=((NY, 16, 128), f32),
    nmw=((NY, 16, 128), f32),
    nm16=((NM, 16, 128), f32),
    nmsib=((NM, 8, 128), f32),
    u=((NX, 128, 128), bf16),
    gps=((64, 512), bf16),
    gpk=((64, 512), f32),
    gpr=((64, 512), bf16),
    gzs=((NZ, 16, 256), bf16),
    gzr=((NZ - 1, 16, 256), bf16),
    gz=((NZ, 16, 256), bf16),
    g4=((2, NX, 64, 512), bf16),
    gb=((512, 512), bf16),
    m0=((512, 512), bf16),
    m1=((512, 512), bf16),
    g2f=((512, 512), f32),
    g2b=((512, 512), bf16),
    sqw=((8, 128), f32),
    big=((2, NX, NM, 128, 128), bf16),
    mb=((2, NX, NY, NM, 16, 128), bf16),
)
PHASES = dict(
    loc=3, sg=1, smo=1, sma=1, x1=3, y1=7, my=7, ay=7, ux=3, gs=1, zr=7, za=7, gx=3, gc=1,
    ax=3, ac=4, ny=8, ns=1, sq=8, sy=8, sx=6, sc=8,
)


def kernel(g, mom, mas, w_out, s_out, nm_out, sq_out, *scratch):
    names = list(BUFFERS)
    B = dict(zip(names, scratch[: len(names)]))
    sems = scratch[len(names):]
    S = {p: (sems[2 * i], sems[2 * i + 1]) for i, p in enumerate(PHASES)}

    d = lax.axis_index("dp")
    z = lax.axis_index("col")
    c = d % 2
    x = (d // 2) % NX
    y = d // 8
    oc = 1 - c
    worker = y < NM

    def dev(yy, xx, cc, zz):
        return ((yy * NX + xx) * 2 + cc, zz)

    sib = dev(y, x, oc, z)

    def xpeer(k):
        return dev(y, (x + k) % NX, c, z)

    def ypeer(k):
        return dev((y + k) % NY, x, c, z)

    def zpeer(k):
        return dev(y, x, c, (z + k) % NZ)

    def remote(phase, i, src, dst, to, send=None):
        return pltpu.make_async_remote_copy(
            src_ref=src,
            dst_ref=dst,
            send_sem=S[phase][0].at[i if send is None else send],
            recv_sem=S[phase][1].at[i],
            device_id=to,
            device_id_type=pl.DeviceIdType.MESH,
        )

    def local(i, src, dst):
        return pltpu.make_async_copy(src, dst, S["loc"][0].at[i])

    def cols(cc):
        return pl.ds(pl.multiple_of(cc * 128, 128), 128)

    def rows8(cc):
        return pl.ds(pl.multiple_of(cc * 8, 8), 8)

    loc = [
        local(0, g.at[:, :, cols(c)], B["own_g"]),
        local(1, mom.at[:, :, cols(c)], B["mom16"].at[:, rows8(c), :]),
        local(2, mas.at[:, :, cols(c)], B["mas16"].at[:, rows8(c), :]),
    ]
    for item in loc:
        item.start()

    barrier = pltpu.get_barrier_semaphore()
    partners = [sib] + [xpeer(k) for k in range(1, NX)]
    partners += [ypeer(k) for k in range(1, NY)] + [zpeer(k) for k in range(1, NZ)]
    for to in partners:
        pl.semaphore_signal(barrier, inc=1, device_id=to, device_id_type=pl.DeviceIdType.MESH)
    pl.semaphore_wait(barrier, len(partners))

    sg = remote("sg", 0, g.at[:, :, cols(oc)], B["sib_g"], sib)
    smo = remote("smo", 0, mom.at[:, :, cols(oc)], B["mom16"].at[:, rows8(c), :], sib)
    sma = remote("sma", 0, mas.at[:, :, cols(oc)], B["mas16"].at[:, rows8(c), :], sib)
    sg.start()
    smo.start()
    sma.start()
    for item in loc:
        item.wait()
    sg.wait_recv()

    def add_pair(k):
        xx = (x + k) % NX

        def one(m, carry):
            for yy in range(NY):
                rows = pl.ds(pl.multiple_of(yy * 64 + xx * 16, 16), 16)
                total = B["own_g"][m, rows, :].astype(f32) + B["sib_g"][m, rows, :].astype(f32)
                B["sum1"][xx, m, pl.ds(yy * 16, 16), :] = total.astype(bf16)
            return carry

        lax.fori_loop(0, NM, one, 0)

    def x1(k):
        return remote("x1", k - 1, B["sum1"].at[(x + k) % NX], B["xr"].at[k - 1], xpeer(k))

    for k in (2, 1, 3):
        add_pair(k)
        x1(k).start()
    add_pair(0)

    smo.wait_recv()
    sma.wait_recv()

    def my(m):
        slot = (m - y + NY) % NY - 1
        return remote("my", slot, B["mom16"].at[m], B["momr"].at[y], dev(m, x, c, z))

    for m in range(NM):
        @pl.when(y != m)
        def _(m=m):
            my(m).start()

        @pl.when(y == m)
        def _(m=m):
            B["momr"][m] = B["mom16"][m]

    B["masb"][...] = B["mas16"][...].astype(bf16)

    for k in range(1, NX):
        x1(k).wait_recv()

    def y1(m):
        slot = (m - y + NY) % NY - 1
        return remote("y1", slot, B["sum2"].at[m], B["yr"].at[slot], dev(m, x, c, z))

    for m in range(NM):
        total = B["sum1"][x, m].astype(f32)
        for k in range(1, NX):
            total = total + B["xr"][k - 1, m].astype(f32)
        B["sum2"][m] = total.astype(bf16)

        @pl.when(y != m)
        def _(m=m):
            y1(m).start()

    def ay(k):
        return remote("ay", k - 1, B["masb"], B["mb"].at[c, x, y], ypeer(k))

    for k in range(1, NY):
        ay(k).start()
    B["mb"][c, x, y] = B["masb"][...]

    def ux(k):
        return remote("ux", k - 1, B["u"].at[x], B["u"].at[x], xpeer(k))

    def ny(yy):
        return remote("ny", y, B["nmw"].at[yy], B["nm16"].at[y], dev(yy, x, c, z), send=yy)

    gs = remote("gs", 0, B["gps"], B["gpr"], sib)

    def zr(k):
        return remote("zr", k - 1, B["gzs"].at[(z + k) % NZ], B["gzr"].at[k - 1], zpeer(k))

    def za(k):
        return remote("za", k - 1, B["gz"].at[z], B["gz"].at[z], zpeer(k))

    def gx(k):
        return remote("gx", k - 1, B["g4"].at[c, x], B["g4"].at[c, x], xpeer(k))

    gc = remote("gc", 0, B["g4"].at[c], B["g4"].at[c], sib)

    def dot(left, right):
        return jnp.dot(left, right, preferred_element_type=f32)

    @pl.when(worker)
    def _():
        for k in range(1, NY):
            pltpu.make_async_remote_copy(
                src_ref=B["mom16"].at[0], dst_ref=B["momr"].at[0],
                send_sem=S["my"][0].at[k - 1], recv_sem=S["my"][1].at[k - 1],
                device_id=sib, device_id_type=pl.DeviceIdType.MESH,
            ).wait_recv()
        for k in range(1, NY):
            pltpu.make_async_remote_copy(
                src_ref=B["sum2"].at[0], dst_ref=B["yr"].at[k - 1],
                send_sem=S["y1"][0].at[k - 1], recv_sem=S["y1"][1].at[k - 1],
                device_id=sib, device_id_type=pl.DeviceIdType.MESH,
            ).wait_recv()
        summed = B["sum2"][y].astype(f32)
        for k in range(1, NY):
            summed = summed + B["yr"][k - 1].astype(f32)
        new_mom = momentum_decay * B["momr"][...].reshape(128, 128) + summed
        B["u"][x] = (summed + momentum_decay * new_mom).astype(bf16)
        for k in (2, 1, 3):
            ux(k).start()
        B["nmw"][...] = new_mom.reshape(NY, 16, 128)
        for yy in range(NY):
            @pl.when(y != yy)
            def _(yy=yy):
                ny(yy).start()

        B["nm16"][y] = B["nmw"][y]
        for k in range(1, NX):
            ux(k).wait_recv()

        full = B["u"][...].reshape(KV, 128)
        part = lax.dot_general(
            B["u"][x], full, (((1,), (1,)), ((), ())), preferred_element_type=f32
        )
        mine = pl.ds(pl.multiple_of(c * 64, 64), 64)
        B["g2f"][0:128, :] = part
        B["gps"][...] = B["g2f"][pl.ds(pl.multiple_of(oc * 64, 64), 64), :].astype(bf16)
        gs.start()
        gs.wait_recv()
        B["gpk"][...] = B["g2f"][mine, :] + B["gpr"][...].astype(f32)
        for p in range(NZ):
            B["gzs"][p] = B["gpk"][
                (p // 2) * 16:(p // 2) * 16 + 16, (p % 2) * 256:(p % 2) * 256 + 256
            ].astype(bf16)
        for k in (4, 3, 5, 2, 6, 1, 7):
            zr(k).start()

    for k in range(1, NY):
        ay(k).wait_recv()

    def ax(k):
        return remote("ax", k - 1, B["mb"].at[c, x], B["mb"].at[c, x], xpeer(k))

    for k in range(1, NX):
        ax(k).start()

    @pl.when(worker)
    def _():
        for k in range(1, NZ):
            zr(k).wait_recv()
        total = B["gzs"][z].astype(f32)
        for k in range(1, NZ):
            total = total + B["gzr"][k - 1].astype(f32)
        B["gz"][z] = total.astype(bf16)
        for k in (4, 3, 5, 2, 6, 1, 7):
            za(k).start()
        for k in range(1, NZ):
            za(k).wait_recv()
        for p in range(NZ):
            B["g4"][
                c, x, (p // 2) * 16:(p // 2) * 16 + 16, (p % 2) * 256:(p % 2) * 256 + 256
            ] = B["gz"][p]
        for k in (2, 1, 3):
            gx(k).start()
        for k in range(1, NX):
            gx(k).wait_recv()
        gc.start()
        gc.wait_recv()

    for k in range(1, NX):
        ax(k).wait_recv()

    def ac(k):
        xx = (x + k) % NX
        return remote("ac", k, B["mb"].at[c, xx], B["mb"].at[c, xx], sib)

    for k in range(NX):
        ac(k).start()

    def sy(yy):
        return remote("sy", y, B["big"].at[c, x, y], B["big"].at[c, x, y], dev(yy, x, c, z), send=yy)

    def sq(yy):
        return remote("sq", y, B["sqw"], sq_out.at[y], dev(yy, x, c, z), send=yy)

    @pl.when(worker)
    def _():
        for xx in range(NX):
            for cc in range(2):
                at = (xx * 2 + cc) * 64
                B["g2f"][at:at + 64, :] = B["g4"][cc, xx].astype(f32)
        gram = B["g2f"][...]
        diagonal = lax.broadcasted_iota(jnp.int32, (512, 512), 0) == lax.broadcasted_iota(
            jnp.int32, (512, 512), 1
        )
        squares = jnp.sum(
            jnp.sum(jnp.where(diagonal, gram, 0.0), axis=0, keepdims=True), axis=1, keepdims=True
        )
        B["sqw"][...] = jnp.broadcast_to(squares, (8, 128))
        for yy in range(NY):
            @pl.when(y != yy)
            def _(yy=yy):
                sq(yy).start()
        sq_out[y] = B["sqw"][...]
        scale = 1.0 / (jnp.sqrt(squares) + epsilon)

        gram = (gram * scale) * scale

        def mixing(gram, half):
            return (quintic_second * gram + quintic_third * dot(half, half)).astype(bf16)

        def advance(gram, half, mix):
            once = quintic_first * gram + dot(mix, half)
            return quintic_first * once + dot(once.astype(bf16), mix)

        B["gb"][...] = gram.astype(bf16)
        B["m0"][...] = mixing(gram, B["gb"][...])
        gram = advance(gram, B["gb"][...], B["m0"][...])
        B["gb"][...] = gram.astype(bf16)
        B["m1"][...] = mixing(gram, B["gb"][...])
        gram = advance(gram, B["gb"][...], B["m1"][...])
        B["g2f"][...] = gram
        B["g2b"][...] = gram.astype(bf16)
        mine = pl.ds(pl.multiple_of(x * 128, 128), 128)
        mix2 = (
            quintic_second * B["g2f"][mine, :]
            + quintic_third * dot(B["g2b"][mine, :], B["g2b"][...])
        ).astype(bf16)
        k1 = quintic_first * (B["m1"][mine, :].astype(f32) + mix2.astype(f32)) + dot(
            mix2, B["m1"][...]
        )
        k0 = (
            quintic_first**2 * B["m0"][mine, :].astype(f32)
            + quintic_first * k1
            + dot(k1.astype(bf16), B["m0"][...])
        )
        last = quintic_first**3 * B["u"][x].astype(f32) + dot(
            k0.astype(bf16), B["u"][...].reshape(KV, 128)
        )
        last = (last * scale).astype(bf16)
        B["big"][c, x, y] = (factor * last.astype(f32)).astype(bf16)
        for k in (4, 3, 5, 2, 6, 1, 7):
            sy((y + k) % NY).start()

    for m in range(NM):
        @pl.when(y != m)
        def _(m=m):
            remote("ny", m, B["nmw"].at[0], B["nm16"].at[m], sib).wait_recv()

    ns = remote("ns", 0, B["nm16"].at[:, rows8(oc), :], B["nmsib"], sib)
    ns.start()
    nm_out[:, :, cols(c)] = B["nm16"][:, rows8(c), :]

    def sx(h, k):
        part = B["big"].at[c, x, pl.ds(h * HALF, HALF)]
        return remote("sx", h * 3 + k - 1, part, part, xpeer(k))

    def sc(h, k):
        part = B["big"].at[c, (x + NX - k) % NX, pl.ds(h * HALF, HALF)]
        return remote("sc", h * 4 + k, part, part, sib)

    for h in range(2):
        for m in range(h * HALF, h * HALF + HALF):
            @pl.when(y != m)
            def _(m=m):
                remote("sy", m, B["big"].at[c, x, m], B["big"].at[c, x, m], sib).wait_recv()
        for k in (2, 1, 3):
            sx(h, k).start()
        sc(h, 0).start()
    ns.wait_recv()
    nm_out[:, :, cols(oc)] = B["nmsib"][...]
    for k in range(NX):
        ac(k).wait_recv()
    for m in range(NM):
        @pl.when(y != m)
        def _(m=m):
            remote("sq", m, B["sqw"], sq_out.at[m], sib).wait_recv()

    def finish(cc, xx, h):
        def one(m, carry):
            for yy in range(NY):
                rows = pl.ds(pl.multiple_of(yy * 64 + xx * 16, 16), 16)
                scaled = B["big"][cc, xx, m, pl.ds(yy * 16, 16), :]
                master = B["mb"][cc, xx, yy, m].astype(f32)
                s_out[m, rows, cols(cc)] = scaled
                w_out[m, rows, cols(cc)] = (
                    master * (1.0 - learn_rate * weight_decay) - learn_rate * scaled.astype(f32)
                ).astype(bf16)
            return carry

        lax.fori_loop(h * HALF, h * HALF + HALF, one, 0)

    for h in range(2):
        for k in (1, 3, 2):
            sx(h, k).wait_recv()
            sc(h, k).start()
    for h in range(2):
        for k in range(NX):
            finish(c, (x + k) % NX, h)
    for h in range(2):
        for k in range(NX):
            sc(h, k).wait_recv()
            finish(oc, (x + NX - k) % NX, h)

    sg.wait_send()
    smo.wait_send()
    sma.wait_send()
    for k in range(1, NX):
        x1(k).wait_send()
        ax(k).wait_send()
    for k in range(1, NY):
        ay(k).wait_send()
    for k in range(NX):
        ac(k).wait_send()
    ns.wait_send()
    for h in range(2):
        for k in range(1, NX):
            sx(h, k).wait_send()
        for k in range(NX):
            sc(h, k).wait_send()
    for m in range(NM):
        @pl.when(y != m)
        def _(m=m):
            my(m).wait_send()
            y1(m).wait_send()

    @pl.when(worker)
    def _():
        for k in range(1, NX):
            ux(k).wait_send()
            gx(k).wait_send()
        gs.wait_send()
        gc.wait_send()
        for k in range(1, NZ):
            zr(k).wait_send()
            za(k).wait_send()
        for yy in range(NY):
            @pl.when(y != yy)
            def _(yy=yy):
                ny(yy).wait_send()
                sq(yy).wait_send()
                sy(yy).wait_send()


def step(g, mom, mas):
    vmem = pl.BlockSpec(memory_space=pltpu.VMEM)
    scratch = [pltpu.VMEM(*spec) for spec in BUFFERS.values()]
    for count in PHASES.values():
        scratch += [pltpu.SemaphoreType.DMA((count,)), pltpu.SemaphoreType.DMA((count,))]
    return pl.pallas_call(
        kernel,
        out_shape=(
            jax.ShapeDtypeStruct((NM, KV, 256), bf16),
            jax.ShapeDtypeStruct((NM, KV, 256), bf16),
            jax.ShapeDtypeStruct((NM, 8, 256), f32),
            jax.ShapeDtypeStruct((NM, 8, 128), f32),
        ),
        in_specs=[pl.BlockSpec(memory_space=pl.ANY), vmem, vmem],
        out_specs=(vmem, vmem, vmem, vmem),
        scratch_shapes=scratch,
        compiler_params=pltpu.CompilerParams(
            collective_id=0, has_side_effects=True, vmem_limit_bytes=48 * 1024 * 1024
        ),
        name="muon_step",
    )(g, mom, mas)


def per_device(gradients, momentum, master, owners):
    new_weights, scaled, new_momentum, squares = step(gradients[0], momentum, master)
    me = lax.axis_index("dp")
    matches = owners[:, None] == owners[None, :]
    order = jnp.arange(NM, dtype=jnp.int32)
    slot = jnp.sum((matches & (order[None, :] < order[:, None])).astype(jnp.int32), axis=1)
    picker = (owners[None, :] == me) & (
        slot[None, :] == jnp.arange(MOST, dtype=jnp.int32)[:, None]
    )
    held = jnp.any(picker, axis=1)
    which = jnp.argmax(picker, axis=1)
    owned = [
        jnp.where(
            held[s], lax.dynamic_index_in_dim(scaled, which[s], 0, keepdims=False), jnp.zeros((), bf16)
        )
        for s in range(MOST)
    ]
    owned_updates = jnp.stack(owned)[None]
    rms = jnp.sqrt(squares[:, 0, 0] / float(KV * D))
    held_rms = jnp.sum(jnp.where(picker, rms[None, :], 0.0), axis=1)[None]
    rows = lax.dynamic_slice_in_dim(scaled, me * 8, 8, axis=1)
    new_master = master * (1.0 - learn_rate * weight_decay) - learn_rate * rows.astype(f32)
    return (new_weights, new_master, new_momentum, owned_updates, held_rms)


def solution(mesh):
    return jax.shard_map(
        per_device,
        mesh=mesh,
        in_specs=(P("dp", None, None, "col"), P(None, "dp", "col"), P(None, "dp", "col"), P()),
        out_specs=(
            P(None, None, "col"),
            P(None, "dp", "col"),
            P(None, "dp", "col"),
            P("dp", None, None, "col"),
            P("dp", None),
        ),
        check_vma=False,
    )
```

```python
import functools
import math

import jax
import jax.numpy as jnp
from jax import lax
from jax.experimental import pallas as pl
from jax.experimental.pallas import tpu as pltpu
from jax.sharding import PartitionSpec as P

KV = 512
D = 2048
NM = 6
MOST = 2
NY = 8
NX = 4
NZ = 8

quintic_first = 3.4445
quintic_second = -4.775
quintic_third = 2.0315
momentum_decay = 0.95
learn_rate = 0.3
weight_decay = 0.1
epsilon = 1e-07
factor = 0.2 * math.sqrt(max(KV, D))

f32 = jnp.float32
bf16 = jnp.bfloat16
ORDER = (0, 3, 1, 4, 2, 5)

BUFFERS = dict(
    own_g=((NM, KV, 128), bf16),
    sib_g=((NM, KV, 128), bf16),
    sum1=((NM, NX, 128, 128), bf16),
    xr=((NM, NX - 1, 128, 128), bf16),
    sum2=((NM, 128, 128), bf16),
    yr=((NY - 1, 128, 128), bf16),
    mas=((NM, 8, 256), f32),
    mom16=((NM, 16, 128), f32),
    mas16=((NM, 16, 128), f32),
    masb=((NM, 16, 128), bf16),
    momr=((NY, 16, 128), f32),
    nmw=((NY, 16, 128), f32),
    nm16=((NM, 16, 128), f32),
    nmsib=((NM, 8, 128), f32),
    u=((NX, 128, 128), bf16),
    part=((128, 512), f32),
    gps=((64, 512), bf16),
    gpr=((64, 512), bf16),
    gzs=((NZ, 16, 256), bf16),
    gzr=((NZ - 1, 16, 256), bf16),
    gz=((NZ, 16, 256), bf16),
    g4=((2, NX, 64, 512), bf16),
    gf=((512, 512), f32),
    gb=((512, 512), bf16),
    m0=((512, 512), bf16),
    m1=((512, 512), bf16),
    sqw=((8, 128), f32),
    sqr=((NM, 8, 128), f32),
    big=((2, NM, NX, 128, 128), bf16),
    mb=((2, NX, NY, NM, 16, 128), bf16),
    w=((NM, KV, 256), bf16),
    ow=((MOST, KV, 256), bf16),
)
PHASES = dict(
    loc=(4, 1), out=(1, 1), sg=(NM, NM), smo=(1, 1), sma=(1, 1), x1=(1, NM), y1=(7, 1), my=(7, 1),
    ay=(1, 1), ux=(1, 1), gs=(1, 1), zr=(1, 1), za=(1, 1), gx=(1, 1), gc=(1, 1), ax=(1, 1),
    ac=(1, 1), ny=(8, NM), ns=(1, 1), sq=(8, NM), sy=(1, NM), sx=(1, NM), sc=(1, NM),
)


def stages(owners, g, mom, mas, w_out, nm_out, ma_out, ow_out, rms_out, *scratch):
    names = list(BUFFERS)
    B = dict(zip(names, scratch[: len(names)]))
    sems = scratch[len(names):]
    S = {p: (sems[2 * i], sems[2 * i + 1]) for i, p in enumerate(PHASES)}
    pending = []

    d = lax.axis_index("dp")
    z = lax.axis_index("col")
    c = d % 2
    x = (d // 2) % NX
    y = d // 8
    oc = 1 - c
    worker = y < NM

    def dev(yy, xx, cc, zz):
        return ((yy * NX + xx) * 2 + cc, zz)

    sib = dev(y, x, oc, z)

    def xpeer(k):
        return dev(y, (x + k) % NX, c, z)

    def ypeer(k):
        return dev((y + k) % NY, x, c, z)

    def zpeer(k):
        return dev(y, x, c, (z + k) % NZ)

    def remote(phase, src, dst, to, send=0, recv=0):
        return pltpu.make_async_remote_copy(
            src_ref=src,
            dst_ref=dst,
            send_sem=S[phase][0].at[send],
            recv_sem=S[phase][1].at[recv],
            device_id=to,
            device_id_type=pl.DeviceIdType.MESH,
        )

    def received(phase, ref, recv=0):
        remote(phase, ref, ref, sib, recv=recv).wait_recv()

    def sent(phase, ref, send=0):
        remote(phase, ref, ref, sib, send=send).wait_send()

    def local(i, src, dst):
        return pltpu.make_async_copy(src, dst, S["loc"][0].at[i])

    def cols(cc):
        return pl.ds(pl.multiple_of(cc * 128, 128), 128)

    def rows8(cc):
        return pl.ds(pl.multiple_of(cc * 8, 8), 8)

    def rows16(at):
        return pl.ds(pl.multiple_of(at * 16, 16), 16)

    def flush():
        for wait in pending:
            wait()
        pending.clear()

    loc = [
        local(0, g.at[:, :, cols(c)], B["own_g"]),
        local(1, mom.at[:, :, cols(c)], B["mom16"].at[:, rows8(c), :]),
        local(2, mas.at[:, :, cols(c)], B["mas16"].at[:, rows8(c), :]),
        local(3, mas, B["mas"]),
    ]
    for item in loc:
        item.start()

    barrier = pltpu.get_barrier_semaphore()
    partners = [sib] + [xpeer(k) for k in range(1, NX)]
    partners += [ypeer(k) for k in range(1, NY)] + [zpeer(k) for k in range(1, NZ)]
    for to in partners:
        pl.semaphore_signal(barrier, inc=1, device_id=to, device_id_type=pl.DeviceIdType.MESH)
    pl.semaphore_wait(barrier, len(partners))
    yield "barrier", flush

    sg = {
        m: remote("sg", g.at[m, :, cols(oc)], B["sib_g"].at[m], sib, send=m, recv=m) for m in ORDER
    }
    smo = remote("smo", mom.at[:, :, cols(oc)], B["mom16"].at[:, rows8(c), :], sib)
    sma = remote("sma", mas.at[:, :, cols(oc)], B["mas16"].at[:, rows8(c), :], sib)
    for m in ORDER:
        sg[m].start()
    smo.start()
    sma.start()
    pending += [sg[m].wait_send for m in ORDER] + [smo.wait_send, sma.wait_send]
    for item in loc:
        item.wait()

    for m in ORDER:
        sg[m].wait_recv()

        def add_pair(xx, carry, m=m):
            for yy in range(NY):
                rows = rows16(yy * 4 + xx)
                total = B["own_g"][m, rows, :].astype(f32) + B["sib_g"][m, rows, :].astype(f32)
                B["sum1"][m, xx, pl.ds(yy * 16, 16), :] = total.astype(bf16)
            return carry

        lax.fori_loop(0, NX, add_pair, 0)
        for k in (2, 1, 3):
            remote(
                "x1", B["sum1"].at[m, (x + k) % NX], B["xr"].at[m, k - 1], xpeer(k), recv=m
            ).start()
    pending.append(lambda: sent("x1", B["xr"]))
    yield "pair", flush

    smo.wait_recv()
    sma.wait_recv()

    def my(m):
        slot = (m - y + NY) % NY - 1
        return remote("my", B["mom16"].at[m], B["momr"].at[y], dev(m, x, c, z), send=slot)

    def y1(m):
        slot = (m - y + NY) % NY - 1
        return remote("y1", B["sum2"].at[m], B["yr"].at[slot], dev(m, x, c, z), send=slot)

    def not_mine(op, m):
        @pl.when(y != m)
        def _():
            op(m)

    for m in ORDER:
        not_mine(lambda m: my(m).start(), m)

        @pl.when(y == m)
        def _(m=m):
            B["momr"][m] = B["mom16"][m]

    B["masb"][...] = B["mas16"][...].astype(bf16)

    for m in ORDER:
        received("x1", B["xr"].at[m], recv=m)
        total = B["sum1"][m, x].astype(f32)
        for k in range(1, NX):
            total = total + B["xr"][m, k - 1].astype(f32)
        B["sum2"][m] = total.astype(bf16)
        not_mine(lambda m: y1(m).start(), m)

    for m in ORDER:
        pending.append(lambda m=m: not_mine(lambda m: my(m).wait_send(), m))
        pending.append(lambda m=m: not_mine(lambda m: y1(m).wait_send(), m))
    yield "x", flush

    for k in range(1, NY):
        remote("ay", B["masb"], B["mb"].at[c, x, y], ypeer(k)).start()
    B["mb"][c, x, y] = B["masb"][...]
    pending.append(lambda: sent("ay", B["mb"].at[c, x, pl.ds(0, NY - 1)]))

    def dot(left, right):
        return jnp.dot(left, right, preferred_element_type=f32)

    def ny(yy):
        return remote(
            "ny", B["nmw"].at[yy], B["nm16"].at[y], dev(yy, x, c, z), send=yy, recv=y
        )

    @pl.when(worker)
    def _():
        received("my", B["momr"].at[pl.ds(0, NY - 1)])
        received("y1", B["yr"])
        summed = B["sum2"][y].astype(f32)
        for k in range(1, NY):
            summed = summed + B["yr"][k - 1].astype(f32)
        new_mom = momentum_decay * B["momr"][...].reshape(128, 128) + summed
        B["u"][x] = (summed + momentum_decay * new_mom).astype(bf16)
        for k in (2, 1, 3):
            remote("ux", B["u"].at[x], B["u"].at[x], xpeer(k)).start()
        B["nmw"][...] = new_mom.reshape(NY, 16, 128)
        B["nm16"][y] = B["nmw"][y]
    yield "y", flush

    @pl.when(worker)
    def _():
        received("ux", B["u"].at[pl.ds(0, NX - 1)])
    yield "ux", flush

    @pl.when(worker)
    def _():
        B["part"][...] = lax.dot_general(
            B["u"][x], B["u"][...].reshape(KV, 128), (((1,), (1,)), ((), ())),
            preferred_element_type=f32,
        )
        B["gps"][...] = B["part"][pl.ds(pl.multiple_of(oc * 64, 64), 64), :].astype(bf16)
        gs = remote("gs", B["gps"], B["gpr"], sib)
        gs.start()
        gs.wait_recv()
        mine = B["part"][pl.ds(pl.multiple_of(c * 64, 64), 64), :] + B["gpr"][...].astype(f32)
        for p in range(NZ):
            at, to = (p // 2) * 16, (p % 2) * 256
            B["gzs"][p] = mine[at:at + 16, to:to + 256].astype(bf16)
        for k in (4, 3, 5, 2, 6, 1, 7):
            remote("zr", B["gzs"].at[(z + k) % NZ], B["gzr"].at[k - 1], zpeer(k)).start()
        for yy in range(NY):
            @pl.when(y != yy)
            def _(yy=yy):
                ny(yy).start()
    yield "gs", flush

    received("ay", B["mb"].at[c, x, pl.ds(0, NY - 1)])
    for k in range(1, NX):
        remote("ax", B["mb"].at[c, x], B["mb"].at[c, x], xpeer(k)).start()
    flush()
    pending.append(lambda: sent("ax", B["mb"].at[c, pl.ds(0, NX - 1)]))

    def drain_head():
        sent("ux", B["u"].at[pl.ds(0, NX - 1)])
        sent("gs", B["gps"])
        sent("zr", B["gzr"])
        for yy in range(NY):
            @pl.when(y != yy)
            def _(yy=yy):
                ny(yy).wait_send()

    pending.append(lambda: pl.when(worker)(drain_head))

    @pl.when(worker)
    def _():
        received("zr", B["gzr"])
        total = B["gzs"][z].astype(f32)
        for k in range(1, NZ):
            total = total + B["gzr"][k - 1].astype(f32)
        B["gz"][z] = total.astype(bf16)
        for k in (4, 3, 5, 2, 6, 1, 7):
            remote("za", B["gz"].at[z], B["gz"].at[z], zpeer(k)).start()
    pending.append(lambda: pl.when(worker)(lambda: sent("za", B["gz"].at[pl.ds(0, NZ - 1)])))
    yield "zr", flush

    @pl.when(worker)
    def _():
        received("za", B["gz"].at[pl.ds(0, NZ - 1)])
        for p in range(NZ):
            at, to = (p // 2) * 16, (p % 2) * 256
            B["g4"][c, x, at:at + 16, to:to + 256] = B["gz"][p]
        for k in (2, 1, 3):
            remote("gx", B["g4"].at[c, x], B["g4"].at[c, x], xpeer(k)).start()
    pending.append(lambda: pl.when(worker)(lambda: sent("gx", B["g4"].at[c, pl.ds(0, NX - 1)])))
    yield "za", flush

    @pl.when(worker)
    def _():
        received("gx", B["g4"].at[c, pl.ds(0, NX - 1)])
        gc = remote("gc", B["g4"].at[c], B["g4"].at[c], sib)
        gc.start()
        gc.wait_recv()
    pending.append(lambda: pl.when(worker)(lambda: sent("gc", B["g4"].at[c])))
    yield "gx", flush

    received("ax", B["mb"].at[c, pl.ds(0, NX - 1)])
    ac = remote("ac", B["mb"].at[c], B["mb"].at[c], sib)
    ac.start()
    pending.append(ac.wait_send)

    def sq(yy):
        return remote("sq", B["sqw"], B["sqr"].at[y], dev(yy, x, c, z), send=yy, recv=y)

    @pl.when(worker)
    def _():
        for xx in range(NX):
            for cc in range(2):
                at = (xx * 2 + cc) * 64
                B["gf"][at:at + 64, :] = B["g4"][cc, xx].astype(f32)
        gram = B["gf"][...]
        diagonal = lax.broadcasted_iota(jnp.int32, (512, 512), 0) == lax.broadcasted_iota(
            jnp.int32, (512, 512), 1
        )
        squares = jnp.sum(
            jnp.sum(jnp.where(diagonal, gram, 0.0), axis=0, keepdims=True), axis=1, keepdims=True
        )
        B["sqw"][...] = jnp.broadcast_to(squares, (8, 128))
        for yy in range(NY):
            @pl.when(y != yy)
            def _(yy=yy):
                sq(yy).start()
        B["sqr"][y] = B["sqw"][...]
        scale = 1.0 / (jnp.sqrt(squares) + epsilon)
        gram = (gram * scale) * scale

        def mixing(gram, half):
            return (quintic_second * gram + quintic_third * dot(half, half)).astype(bf16)

        def advance(gram, half, mix):
            once = quintic_first * gram + dot(mix, half)
            return quintic_first * once + dot(once.astype(bf16), mix)

        B["gb"][...] = gram.astype(bf16)
        B["m0"][...] = mixing(gram, B["gb"][...])
        gram = advance(gram, B["gb"][...], B["m0"][...])
        B["gb"][...] = gram.astype(bf16)
        B["m1"][...] = mixing(gram, B["gb"][...])
        gram = advance(gram, B["gb"][...], B["m1"][...])
        B["gf"][...] = gram
        B["gb"][...] = gram.astype(bf16)
        mine = pl.ds(pl.multiple_of(x * 128, 128), 128)
        mix2 = (
            quintic_second * B["gf"][mine, :]
            + quintic_third * dot(B["gb"][mine, :], B["gb"][...])
        ).astype(bf16)
        k1 = quintic_first * (B["m1"][mine, :].astype(f32) + mix2.astype(f32)) + dot(
            mix2, B["m1"][...]
        )
        k0 = (
            quintic_first**2 * B["m0"][mine, :].astype(f32)
            + quintic_first * k1
            + dot(k1.astype(bf16), B["m0"][...])
        )
        last = quintic_first**3 * B["u"][x].astype(f32) + dot(
            k0.astype(bf16), B["u"][...].reshape(KV, 128)
        )
        last = (last * scale).astype(bf16)
        B["big"][c, y, x] = (factor * last.astype(f32)).astype(bf16)
    yield "ns", flush

    @pl.when(worker)
    def _():
        for k in (4, 3, 5, 2, 6, 1, 7):
            remote("sy", B["big"].at[c, y, x], B["big"].at[c, y, x], ypeer(k), recv=y).start()

    def drain_worker():
        sent("sy", B["yr"])
        for yy in range(NY):
            @pl.when(y != yy)
            def _(yy=yy):
                sq(yy).wait_send()

    for m in range(NM):
        not_mine(lambda m: received("ny", B["nm16"].at[m], recv=m), m)
    ns = remote("ns", B["nm16"].at[:, rows8(oc), :], B["nmsib"], sib)
    ns.start()
    pending.append(ns.wait_send)
    nm_out[:, :, cols(c)] = B["nm16"][:, rows8(c), :]
    ac.wait_recv()
    flush()
    ns.wait_recv()
    nm_out[:, :, cols(oc)] = B["nmsib"][...]

    for m in ORDER:
        not_mine(lambda m: received("sy", B["big"].at[c, m, x], recv=m), m)
        for k in (2, 1, 3):
            remote("sx", B["big"].at[c, m, x], B["big"].at[c, m, x], xpeer(k), recv=m).start()
    pending.append(lambda: pl.when(worker)(drain_worker))
    pending.append(lambda: sent("sx", B["xr"]))
    yield "sy", flush

    ids = [owners[m] for m in range(NM)]
    slots = [sum([(ids[j] == ids[m]).astype(jnp.int32) for j in range(m)], jnp.int32(0)) for m in range(NM)]
    picks = [[(ids[m] == d) & (slots[m] == s) for m in range(NM)] for s in range(MOST)]

    def finish(cc, m, first):
        def one(xx, carry):
            for yy in range(NY):
                rows = rows16(yy * 4 + xx)
                scaled = B["big"][cc, m, xx, pl.ds(yy * 16, 16), :]
                master = B["mb"][cc, xx, yy, m].astype(f32)
                B["w"][m, rows, cols(cc)] = (
                    master * (1.0 - learn_rate * weight_decay) - learn_rate * scaled.astype(f32)
                ).astype(bf16)
                for s in range(MOST):
                    before = jnp.zeros_like(scaled) if first else B["ow"][s, rows, cols(cc)]
                    B["ow"][s, rows, cols(cc)] = jnp.where(picks[s][m], scaled, before)
            return carry

        lax.fori_loop(0, NX, one, 0)
        own = B["big"][cc, m, x, pl.ds(pl.multiple_of(y * 16, 16), 16), :].astype(f32)
        own = jnp.where(c == 0, own[0:8], own[8:16])
        ma_out[m, :, cols(cc)] = (
            B["mas"][m, :, cols(cc)] * (1.0 - learn_rate * weight_decay) - learn_rate * own
        )

    for m in ORDER:
        received("sx", B["big"].at[c, m, pl.ds(0, NX - 1)], recv=m)
        remote("sc", B["big"].at[c, m], B["big"].at[c, m], sib, recv=m).start()
        finish(c, m, m == ORDER[0])
    pending.append(lambda: sent("sc", B["big"].at[c]))
    yield "sx", flush

    for m in range(NM):
        not_mine(lambda m: received("sq", B["sqr"].at[m], recv=m), m)
    lane = lax.broadcasted_iota(jnp.int32, (1, 128), 1)
    rms = jnp.zeros((1, 128), f32)
    for m in range(NM):
        value = jnp.sqrt(B["sqr"][m, 0:1, :] / float(KV * D))
        for s in range(MOST):
            rms = rms + jnp.where(picks[s][m] & (lane == s), value, 0.0)
    rms_out[...] = rms[:, 0:MOST]
    done = []
    for m in ORDER:
        received("sc", B["big"].at[oc, m], recv=m)
        finish(oc, m, m == ORDER[0])
        pltpu.make_async_copy(B["w"].at[m], w_out.at[m], S["out"][0].at[0]).start()
    out = pltpu.make_async_copy(B["ow"], ow_out, S["out"][1].at[0])
    out.start()
    flush()
    pltpu.make_async_copy(B["w"], w_out, S["out"][0].at[0]).wait()
    out.wait()


def kernel(stop, *refs):
    for name, flush in stages(*refs):
        if name == stop:
            flush()
            break


def step(owners, g, mom, mas, stop=None, collective_id=0):
    vmem = pl.BlockSpec(memory_space=pltpu.VMEM)
    anywhere = pl.BlockSpec(memory_space=pl.ANY)
    scratch = [pltpu.VMEM(*spec) for spec in BUFFERS.values()]
    for send, recv in PHASES.values():
        scratch += [pltpu.SemaphoreType.DMA((send,)), pltpu.SemaphoreType.DMA((recv,))]
    return pl.pallas_call(
        functools.partial(kernel, stop),
        out_shape=(
            jax.ShapeDtypeStruct((NM, KV, 256), bf16),
            jax.ShapeDtypeStruct((NM, 8, 256), f32),
            jax.ShapeDtypeStruct((NM, 8, 256), f32),
            jax.ShapeDtypeStruct((MOST, KV, 256), bf16),
            jax.ShapeDtypeStruct((1, MOST), f32),
        ),
        in_specs=[pl.BlockSpec(memory_space=pltpu.SMEM), anywhere, anywhere, anywhere],
        out_specs=(anywhere, vmem, vmem, anywhere, vmem),
        scratch_shapes=scratch,
        compiler_params=pltpu.CompilerParams(
            collective_id=collective_id, has_side_effects=True, vmem_limit_bytes=60 * 1024 * 1024
        ),
        name="muon_step",
    )(owners, g, mom, mas)


def per_device(gradients, momentum, master, owners):
    new_weights, new_momentum, new_master, owned_updates, owned_rms = step(
        owners, gradients[0], momentum, master
    )
    return (new_weights, new_master, new_momentum, owned_updates[None], owned_rms)


def solution(mesh):
    return jax.shard_map(
        per_device,
        mesh=mesh,
        in_specs=(P("dp", None, None, "col"), P(None, "dp", "col"), P(None, "dp", "col"), P()),
        out_specs=(
            P(None, None, "col"),
            P(None, "dp", "col"),
            P(None, "dp", "col"),
            P("dp", None, None, "col"),
            P("dp", None),
        ),
        check_vma=False,
    )
```

```python
import functools
import math

import jax
import jax.numpy as jnp
from jax import lax
from jax.experimental import pallas as pl
from jax.experimental.pallas import tpu as pltpu
from jax.sharding import PartitionSpec as P

KV = 512
D = 2048
NM = 6
MOST = 2
NY = 8
NX = 4
NZ = 8

quintic_first = 3.4445
quintic_second = -4.775
quintic_third = 2.0315
momentum_decay = 0.95
learn_rate = 0.3
weight_decay = 0.1
epsilon = 1e-07
factor = 0.2 * math.sqrt(max(KV, D))

f32 = jnp.float32
bf16 = jnp.bfloat16
FAR = (4, 3, 5, 2, 6, 1, 7, 0)
NEAR = (0, 1, 7, 2, 6, 3, 5, 4)

BUFFERS = dict(
    own_g=((NM, KV, 128), bf16),
    sib_g=((NM, KV, 128), bf16),
    sum1=((NM, NX, 128, 128), bf16),
    xr=((NM, NX - 1, 128, 128), bf16),
    sum2=((NM, 128, 128), bf16),
    yr=((NY - 1, 128, 128), bf16),
    mas=((NM, 8, 256), f32),
    mom16=((NM, 16, 128), f32),
    mas16=((NM, 16, 128), f32),
    masb=((NM, 16, 128), bf16),
    momr=((NY, 16, 128), f32),
    nmw=((NY, 16, 128), f32),
    nm16=((NM, 16, 128), f32),
    nmsib=((NM, 8, 128), f32),
    u=((NX, 128, 128), bf16),
    part=((128, 512), f32),
    gps=((64, 512), bf16),
    gpr=((64, 512), bf16),
    gzs=((NZ, 16, 256), bf16),
    gzr=((NZ - 1, 16, 256), bf16),
    gz=((NZ, 16, 256), bf16),
    g4=((2, NX, 64, 512), bf16),
    gf=((512, 512), f32),
    gb=((512, 512), bf16),
    m0=((512, 512), bf16),
    m1=((512, 512), bf16),
    sqw=((8, 128), f32),
    sqr=((NM, 8, 128), f32),
    big=((2, NM, NX, 128, 128), bf16),
    mb=((2, NX, NY, NM, 16, 128), bf16),
)
PHASES = dict(
    loc=(4, 1), sg=(1, NM), smo=(1, 1), sma=(1, 1), x1=(1, NM), y1=(7, 1), my=(7, 1),
    ay=(1, 1), ux=(1, 1), gs=(1, 1), zr=(1, 1), za=(1, 1), gx=(1, 1), gc=(1, 1), ax=(1, 1),
    ac=(1, 1), ny=(8, NM), ns=(1, 1), sq=(8, NM), sy=(1, NM), sx=(1, NM), sc=(1, NM),
)


def stages(owners, g, mom, mas, w_out, nm_out, ma_out, ow_out, rms_out, *scratch):
    names = list(BUFFERS)
    B = dict(zip(names, scratch[: len(names)]))
    sems = scratch[len(names):]
    S = {p: (sems[2 * i], sems[2 * i + 1]) for i, p in enumerate(PHASES)}
    pending = []

    d = lax.axis_index("dp")
    z = lax.axis_index("col")
    c = d % 2
    x = (d // 2) % NX
    y = d // 8
    oc = 1 - c
    worker = y < NM

    def dev(yy, xx, cc, zz):
        return ((yy * NX + xx) * 2 + cc, zz)

    sib = dev(y, x, oc, z)

    def xpeer(k):
        return dev(y, (x + k) % NX, c, z)

    def ypeer(k):
        return dev((y + k) % NY, x, c, z)

    def zpeer(k):
        return dev(y, x, c, (z + k) % NZ)

    def remote(phase, src, dst, to, send=0, recv=0):
        return pltpu.make_async_remote_copy(
            src_ref=src,
            dst_ref=dst,
            send_sem=S[phase][0].at[send],
            recv_sem=S[phase][1].at[recv],
            device_id=to,
            device_id_type=pl.DeviceIdType.MESH,
        )

    def received(phase, ref, recv=0):
        remote(phase, ref, ref, sib, recv=recv).wait_recv()

    def sent(phase, ref, send=0):
        remote(phase, ref, ref, sib, send=send).wait_send()

    def local(i, src, dst):
        return pltpu.make_async_copy(src, dst, S["loc"][0].at[i])

    def cols(cc):
        return pl.ds(pl.multiple_of(cc * 128, 128), 128)

    def rows8(cc):
        return pl.ds(pl.multiple_of(cc * 8, 8), 8)

    def rows16(at):
        return pl.ds(pl.multiple_of(at * 16, 16), 16)

    def flush():
        for wait in pending:
            wait()
        pending.clear()

    loc = [
        local(0, g.at[:, :, cols(c)], B["own_g"]),
        local(1, mom.at[:, :, cols(c)], B["mom16"].at[:, rows8(c), :]),
        local(2, mas.at[:, :, cols(c)], B["mas16"].at[:, rows8(c), :]),
        local(3, mas, B["mas"]),
    ]
    for item in loc:
        item.start()

    barrier = pltpu.get_barrier_semaphore()
    partners = [sib] + [xpeer(k) for k in range(1, NX)]
    partners += [ypeer(k) for k in range(1, NY)] + [zpeer(k) for k in range(1, NZ)]
    for to in partners:
        pl.semaphore_signal(barrier, inc=1, device_id=to, device_id_type=pl.DeviceIdType.MESH)
    pl.semaphore_wait(barrier, len(partners))
    ow_out[...] = jnp.zeros_like(ow_out)
    yield "barrier", flush

    def each(order, op):
        for delta in order:
            m = (y + delta) % NY
            pl.when(m < NM)(functools.partial(op, m, delta))

    smo = remote("smo", mom.at[:, :, cols(oc)], B["mom16"].at[:, rows8(c), :], sib)
    sma = remote("sma", mas.at[:, :, cols(oc)], B["mas16"].at[:, rows8(c), :], sib)
    smo.start()
    sma.start()

    def swap(m, delta):
        remote("sg", g.at[m, :, cols(oc)], B["sib_g"].at[m], sib, recv=m).start()

    each(FAR, swap)
    pending += [lambda: sent("sg", B["sib_g"]), smo.wait_send, sma.wait_send]
    for item in loc:
        item.wait()

    def pair(m, delta):
        received("sg", B["sib_g"].at[m], recv=m)

        def add(xx, carry):
            for yy in range(NY):
                rows = rows16(yy * 4 + xx)
                total = B["own_g"][m, rows, :].astype(f32) + B["sib_g"][m, rows, :].astype(f32)
                B["sum1"][m, xx, pl.ds(yy * 16, 16), :] = total.astype(bf16)
            return carry

        lax.fori_loop(0, NX, add, 0)
        for k in (2, 1, 3):
            remote(
                "x1", B["sum1"].at[m, (x + k) % NX], B["xr"].at[m, k - 1], xpeer(k), recv=m
            ).start()

    each(FAR, pair)
    pending.append(lambda: sent("x1", B["xr"]))
    yield "pair", flush

    smo.wait_recv()
    sma.wait_recv()

    def my(m):
        slot = (m - y + NY) % NY - 1
        return remote("my", B["mom16"].at[m], B["momr"].at[y], dev(m, x, c, z), send=slot)

    def y1(m):
        slot = (m - y + NY) % NY - 1
        return remote("y1", B["sum2"].at[m], B["yr"].at[slot], dev(m, x, c, z), send=slot)

    def not_mine(op, m):
        @pl.when(y != m)
        def _():
            op(m)

    for m in range(NM):
        not_mine(lambda m: my(m).start(), m)

        @pl.when(y == m)
        def _(m=m):
            B["momr"][m] = B["mom16"][m]

    B["masb"][...] = B["mas16"][...].astype(bf16)
    for k in (4, 3, 5, 2, 6, 1, 7):
        remote("ay", B["masb"], B["mb"].at[c, x, y], ypeer(k)).start()
    B["mb"][c, x, y] = B["masb"][...]
    pending.append(lambda: sent("ay", B["mb"].at[c, x, pl.ds(0, NY - 1)]))

    def along_x(m, delta):
        received("x1", B["xr"].at[m], recv=m)
        total = B["sum1"][m, x].astype(f32)
        for k in range(1, NX):
            total = total + B["xr"][m, k - 1].astype(f32)
        B["sum2"][m] = total.astype(bf16)
        if delta:
            y1(m).start()

    each(FAR, along_x)
    for m in range(NM):
        pending.append(lambda m=m: not_mine(lambda m: my(m).wait_send(), m))
        pending.append(lambda m=m: not_mine(lambda m: y1(m).wait_send(), m))
    yield "x", flush

    def dot(left, right):
        return jnp.dot(left, right, preferred_element_type=f32)

    def ny(yy):
        return remote(
            "ny", B["nmw"].at[yy], B["nm16"].at[y], dev(yy, x, c, z), send=yy, recv=y
        )

    @pl.when(worker)
    def _():
        received("my", B["momr"].at[pl.ds(0, NY - 1)])
        received("y1", B["yr"])
        summed = B["sum2"][y].astype(f32)
        for k in range(1, NY):
            summed = summed + B["yr"][k - 1].astype(f32)
        new_mom = momentum_decay * B["momr"][...].reshape(128, 128) + summed
        B["u"][x] = (summed + momentum_decay * new_mom).astype(bf16)
        for k in (2, 1, 3):
            remote("ux", B["u"].at[x], B["u"].at[x], xpeer(k)).start()
        B["nmw"][...] = new_mom.reshape(NY, 16, 128)
        B["nm16"][y] = B["nmw"][y]
    yield "y", flush

    @pl.when(worker)
    def _():
        received("ux", B["u"].at[pl.ds(0, NX - 1)])
    yield "ux", flush

    @pl.when(worker)
    def _():
        B["part"][...] = lax.dot_general(
            B["u"][x], B["u"][...].reshape(KV, 128), (((1,), (1,)), ((), ())),
            preferred_element_type=f32,
        )
        B["gps"][...] = B["part"][pl.ds(pl.multiple_of(oc * 64, 64), 64), :].astype(bf16)
        gs = remote("gs", B["gps"], B["gpr"], sib)
        gs.start()
        gs.wait_recv()
        mine = B["part"][pl.ds(pl.multiple_of(c * 64, 64), 64), :] + B["gpr"][...].astype(f32)
        for p in range(NZ):
            at, to = (p // 2) * 16, (p % 2) * 256
            B["gzs"][p] = mine[at:at + 16, to:to + 256].astype(bf16)
        for k in (4, 3, 5, 2, 6, 1, 7):
            remote("zr", B["gzs"].at[(z + k) % NZ], B["gzr"].at[k - 1], zpeer(k)).start()
        for yy in range(NY):
            @pl.when(y != yy)
            def _(yy=yy):
                ny(yy).start()
    yield "gs", flush

    received("ay", B["mb"].at[c, x, pl.ds(0, NY - 1)])
    for k in range(1, NX):
        remote("ax", B["mb"].at[c, x], B["mb"].at[c, x], xpeer(k)).start()
    flush()
    pending.append(lambda: sent("ax", B["mb"].at[c, pl.ds(0, NX - 1)]))

    def drain_head():
        sent("ux", B["u"].at[pl.ds(0, NX - 1)])
        sent("gs", B["gps"])
        sent("zr", B["gzr"])
        for yy in range(NY):
            @pl.when(y != yy)
            def _(yy=yy):
                ny(yy).wait_send()

    pending.append(lambda: pl.when(worker)(drain_head))

    @pl.when(worker)
    def _():
        received("zr", B["gzr"])
        total = B["gzs"][z].astype(f32)
        for k in range(1, NZ):
            total = total + B["gzr"][k - 1].astype(f32)
        B["gz"][z] = total.astype(bf16)
        for k in (4, 3, 5, 2, 6, 1, 7):
            remote("za", B["gz"].at[z], B["gz"].at[z], zpeer(k)).start()
    pending.append(lambda: pl.when(worker)(lambda: sent("za", B["gz"].at[pl.ds(0, NZ - 1)])))
    yield "zr", flush

    @pl.when(worker)
    def _():
        received("za", B["gz"].at[pl.ds(0, NZ - 1)])
        for p in range(NZ):
            at, to = (p // 2) * 16, (p % 2) * 256
            B["g4"][c, x, at:at + 16, to:to + 256] = B["gz"][p]
        for k in (2, 1, 3):
            remote("gx", B["g4"].at[c, x], B["g4"].at[c, x], xpeer(k)).start()
    pending.append(lambda: pl.when(worker)(lambda: sent("gx", B["g4"].at[c, pl.ds(0, NX - 1)])))
    yield "za", flush

    @pl.when(worker)
    def _():
        received("gx", B["g4"].at[c, pl.ds(0, NX - 1)])
        gc = remote("gc", B["g4"].at[c], B["g4"].at[c], sib)
        gc.start()
        gc.wait_recv()
    pending.append(lambda: pl.when(worker)(lambda: sent("gc", B["g4"].at[c])))
    yield "gx", flush

    received("ax", B["mb"].at[c, pl.ds(0, NX - 1)])
    ac = remote("ac", B["mb"].at[c], B["mb"].at[c], sib)
    ac.start()
    pending.append(ac.wait_send)

    def sq(yy):
        return remote("sq", B["sqw"], B["sqr"].at[y], dev(yy, x, c, z), send=yy, recv=y)

    @pl.when(worker)
    def _():
        row = lax.broadcasted_iota(jnp.int32, (64, 128), 0)
        col = lax.broadcasted_iota(jnp.int32, (64, 128), 1)
        squares = jnp.zeros((64, 128), f32)
        for xx in range(NX):
            for cc in range(2):
                block = B["g4"][cc, xx, :, xx * 128:xx * 128 + 128].astype(f32)
                squares = squares + jnp.where(row + cc * 64 == col, block, 0.0)
        squares = jnp.sum(jnp.sum(squares, axis=0, keepdims=True), axis=1, keepdims=True)
        B["sqw"][...] = jnp.broadcast_to(squares, (8, 128))
        for yy in range(NY):
            @pl.when(y != yy)
            def _(yy=yy):
                sq(yy).start()
        B["sqr"][y] = B["sqw"][...]
        scale = 1.0 / (jnp.sqrt(squares) + epsilon)
        for xx in range(NX):
            for cc in range(2):
                at = (xx * 2 + cc) * 64
                B["gf"][at:at + 64, :] = (B["g4"][cc, xx].astype(f32) * scale) * scale
        gram = B["gf"][...]

        def mixing(gram, half):
            return (quintic_second * gram + quintic_third * dot(half, half)).astype(bf16)

        def advance(gram, half, mix):
            once = quintic_first * gram + dot(mix, half)
            return quintic_first * once + dot(once.astype(bf16), mix)

        B["gb"][...] = gram.astype(bf16)
        B["m0"][...] = mixing(gram, B["gb"][...])
        gram = advance(gram, B["gb"][...], B["m0"][...])
        B["gb"][...] = gram.astype(bf16)
        B["m1"][...] = mixing(gram, B["gb"][...])
        gram = advance(gram, B["gb"][...], B["m1"][...])
        B["gf"][...] = gram
        B["gb"][...] = gram.astype(bf16)
        mine = pl.ds(pl.multiple_of(x * 128, 128), 128)
        mix2 = (
            quintic_second * B["gf"][mine, :]
            + quintic_third * dot(B["gb"][mine, :], B["gb"][...])
        ).astype(bf16)
        k1 = quintic_first * (B["m1"][mine, :].astype(f32) + mix2.astype(f32)) + dot(
            mix2, B["m1"][...]
        )
        k0 = (
            quintic_first**2 * B["m0"][mine, :].astype(f32)
            + quintic_first * k1
            + dot(k1.astype(bf16), B["m0"][...])
        )
        last = quintic_first**3 * B["u"][x].astype(f32) + dot(
            k0.astype(bf16), B["u"][...].reshape(KV, 128)
        )
        last = (last * scale).astype(bf16)
        B["big"][c, y, x] = (factor * last.astype(f32)).astype(bf16)
    yield "ns", flush

    @pl.when(worker)
    def _():
        for k in (4, 3, 5, 2, 6, 1, 7):
            remote("sy", B["big"].at[c, y, x], B["big"].at[c, y, x], ypeer(k), recv=y).start()

    def drain_worker():
        sent("sy", B["yr"])
        for yy in range(NY):
            @pl.when(y != yy)
            def _(yy=yy):
                sq(yy).wait_send()

    for m in range(NM):
        not_mine(lambda m: received("ny", B["nm16"].at[m], recv=m), m)
    ns = remote("ns", B["nm16"].at[:, rows8(oc), :], B["nmsib"], sib)
    ns.start()
    pending.append(ns.wait_send)
    nm_out[:, :, cols(c)] = B["nm16"][:, rows8(c), :]
    ac.wait_recv()
    flush()
    ns.wait_recv()
    nm_out[:, :, cols(oc)] = B["nmsib"][...]

    def on_x(m, delta):
        if delta:
            received("sy", B["big"].at[c, m, x], recv=m)
        for k in (2, 1, 3):
            remote("sx", B["big"].at[c, m, x], B["big"].at[c, m, x], xpeer(k), recv=m).start()

    each(NEAR, on_x)
    pending.append(lambda: pl.when(worker)(drain_worker))
    pending.append(lambda: sent("sx", B["xr"]))
    yield "sy", flush

    def picks(m):
        mine = owners[m]
        slot = jnp.int32(0)
        for j in range(NM):
            slot = slot + ((owners[j] == mine) & (j < m)).astype(jnp.int32)
        return [(mine == d) & (slot == s) for s in range(MOST)]

    def finish(cc, m):
        chosen = picks(m)

        def one(xx, carry):
            for yy in range(NY):
                rows = rows16(yy * 4 + xx)
                scaled = B["big"][cc, m, xx, pl.ds(yy * 16, 16), :]
                master = B["mb"][cc, xx, yy, m].astype(f32)
                w_out[m, rows, cols(cc)] = (
                    master * (1.0 - learn_rate * weight_decay) - learn_rate * scaled.astype(f32)
                ).astype(bf16)
                for s in range(MOST):
                    ow_out[s, rows, cols(cc)] = jnp.where(
                        chosen[s], scaled, ow_out[s, rows, cols(cc)]
                    )
            return carry

        lax.fori_loop(0, NX, one, 0)
        own = B["big"][cc, m, x, pl.ds(pl.multiple_of(y * 16, 16), 16), :].astype(f32)
        own = jnp.where(c == 0, own[0:8], own[8:16])
        ma_out[m, :, cols(cc)] = (
            B["mas"][m, :, cols(cc)] * (1.0 - learn_rate * weight_decay) - learn_rate * own
        )

    def to_sibling(m, delta):
        received("sx", B["big"].at[c, m, pl.ds(0, NX - 1)], recv=m)
        remote("sc", B["big"].at[c, m], B["big"].at[c, m], sib, recv=m).start()
        finish(c, m)

    each(NEAR, to_sibling)
    pending.append(lambda: sent("sc", B["big"].at[c]))
    yield "sx", flush

    for m in range(NM):
        not_mine(lambda m: received("sq", B["sqr"].at[m], recv=m), m)
    lane = lax.broadcasted_iota(jnp.int32, (1, 128), 1)
    rms = jnp.zeros((1, 128), f32)
    for m in range(NM):
        value = jnp.sqrt(B["sqr"][m, 0:1, :] / float(KV * D))
        chosen = picks(m)
        for s in range(MOST):
            rms = rms + jnp.where(chosen[s] & (lane == s), value, 0.0)
    rms_out[...] = rms[:, 0:MOST]

    def from_sibling(m, delta):
        received("sc", B["big"].at[oc, m], recv=m)
        finish(oc, m)

    each(NEAR, from_sibling)
    flush()


def kernel(stop, *refs):
    for name, flush in stages(*refs):
        if name == stop:
            flush()
            break


def step(owners, g, mom, mas, stop=None, collective_id=0):
    vmem = pl.BlockSpec(memory_space=pltpu.VMEM)
    hbm = pl.BlockSpec(memory_space=pltpu.HBM)
    scratch = [pltpu.VMEM(*spec) for spec in BUFFERS.values()]
    for send, recv in PHASES.values():
        scratch += [pltpu.SemaphoreType.DMA((send,)), pltpu.SemaphoreType.DMA((recv,))]
    return pl.pallas_call(
        functools.partial(kernel, stop),
        out_shape=(
            pltpu.VMEM((NM, KV, 256), bf16),
            pltpu.VMEM((NM, 8, 256), f32),
            pltpu.VMEM((NM, 8, 256), f32),
            pltpu.VMEM((MOST, KV, 256), bf16),
            pltpu.VMEM((1, MOST), f32),
        ),
        in_specs=[pl.BlockSpec(memory_space=pltpu.SMEM), hbm, hbm, hbm],
        out_specs=(vmem, vmem, vmem, vmem, vmem),
        scratch_shapes=scratch,
        compiler_params=pltpu.CompilerParams(
            collective_id=collective_id, has_side_effects=True, vmem_limit_bytes=40 * 1024 * 1024
        ),
        name="muon_step",
    )(*(pltpu.with_memory_space_constraint(item, pltpu.HBM) for item in (owners, g, mom, mas)))


def copy_kernel(*refs):
    count = (len(refs) - 1) // 2
    copies = [
        pltpu.make_async_copy(refs[i], refs[count + i], refs[-1].at[i]) for i in range(count)
    ]
    for copy in copies:
        copy.start()
    for copy in copies:
        copy.wait()


def write_out(arrays):
    return pl.pallas_call(
        copy_kernel,
        out_shape=[jax.ShapeDtypeStruct(item.shape, item.dtype) for item in arrays],
        in_specs=[pl.BlockSpec(memory_space=pl.ANY)] * len(arrays),
        out_specs=[pl.BlockSpec(memory_space=pl.ANY)] * len(arrays),
        scratch_shapes=[pltpu.SemaphoreType.DMA((len(arrays),))],
        name="write_out",
    )(*(pltpu.with_memory_space_constraint(item, pltpu.VMEM) for item in arrays))


def per_device(gradients, momentum, master, owners):
    new_weights, new_momentum, new_master, owned_updates, owned_rms = write_out(
        step(owners, gradients[0], momentum, master)
    )
    return (new_weights, new_master, new_momentum, owned_updates[None], owned_rms)


def solution(mesh):
    return jax.shard_map(
        per_device,
        mesh=mesh,
        in_specs=(P("dp", None, None, "col"), P(None, "dp", "col"), P(None, "dp", "col"), P()),
        out_specs=(
            P(None, None, "col"),
            P(None, "dp", "col"),
            P(None, "dp", "col"),
            P("dp", None, None, "col"),
            P("dp", None),
        ),
        check_vma=False,
    )
```

```python
import functools
import math

import jax
import jax.numpy as jnp
from jax import lax
from jax.experimental import pallas as pl
from jax.experimental.pallas import tpu as pltpu
from jax.sharding import PartitionSpec as P

KV = 512
D = 2048
NM = 6
MOST = 2
NY = 8
NX = 4
NZ = 8

quintic_first = 3.4445
quintic_second = -4.775
quintic_third = 2.0315
momentum_decay = 0.95
learn_rate = 0.3
weight_decay = 0.1
epsilon = 1e-07
factor = 0.2 * math.sqrt(max(KV, D))

f32 = jnp.float32
bf16 = jnp.bfloat16
FAR = (4, 3, 5, 2, 6, 1, 7, 0)
NEAR = (0, 1, 7, 2, 6, 3, 5, 4)

BUFFERS = dict(
    gv=((NM, KV, 256), bf16),
    sib_g=((NM, KV, 128), bf16),
    sum1=((NM, NX, 128, 128), bf16),
    xr=((NM, NX - 1, 128, 128), bf16),
    sum2=((NM, 128, 128), bf16),
    yr=((NY - 1, 128, 128), bf16),
    mas=((NM, 8, 256), f32),
    mom16=((NM, 16, 128), f32),
    mas16=((NM, 16, 128), f32),
    masb=((NM, 16, 128), bf16),
    momr=((NY, 16, 128), f32),
    nmw=((NY, 16, 128), f32),
    nm16=((NM, 16, 128), f32),
    nmsib=((NM, 8, 128), f32),
    u=((NX, 128, 128), bf16),
    part=((128, 512), f32),
    gps=((64, 512), bf16),
    gpr=((64, 512), bf16),
    gzs=((NZ, 16, 256), bf16),
    gzr=((NZ - 1, 16, 256), bf16),
    gz=((NZ, 16, 256), bf16),
    g4=((2, NX, 64, 512), bf16),
    gf=((512, 512), f32),
    gb=((512, 512), bf16),
    m0=((512, 512), bf16),
    m1=((512, 512), bf16),
    sqw=((8, 128), f32),
    sqr=((NM, 8, 128), f32),
    big=((2, NM, NX, 128, 128), bf16),
    mb=((2, NX, NY, NM, 16, 128), bf16),
)
PHASES = dict(
    loc=(4, 1), sg=(1, NM), smo=(1, 1), sma=(1, 1), x1=(1, NM), y1=(7, 1), my=(7, 1),
    ay=(1, 1), ux=(1, 1), gs=(1, 1), zr=(1, 1), za=(1, 1), gx=(1, 1), gc=(1, 1), ax=(1, 1),
    ac=(1, 1), ny=(8, NM), ns=(1, 1), sq=(8, NM), sy=(1, NM), sx=(1, NM), sc=(1, NM),
)


def stages(owners, g, mom, mas, w_out, nm_out, ma_out, ow_out, rms_out, *scratch):
    names = list(BUFFERS)
    B = dict(zip(names, scratch[: len(names)]))
    sems = scratch[len(names):]
    S = {p: (sems[2 * i], sems[2 * i + 1]) for i, p in enumerate(PHASES)}
    pending = []

    d = lax.axis_index("dp")
    z = lax.axis_index("col")
    c = d % 2
    x = (d // 2) % NX
    y = d // 8
    oc = 1 - c
    worker = y < NM

    def dev(yy, xx, cc, zz):
        return ((yy * NX + xx) * 2 + cc, zz)

    sib = dev(y, x, oc, z)

    def xpeer(k):
        return dev(y, (x + k) % NX, c, z)

    def ypeer(k):
        return dev((y + k) % NY, x, c, z)

    def zpeer(k):
        return dev(y, x, c, (z + k) % NZ)

    def remote(phase, src, dst, to, send=0, recv=0):
        return pltpu.make_async_remote_copy(
            src_ref=src,
            dst_ref=dst,
            send_sem=S[phase][0].at[send],
            recv_sem=S[phase][1].at[recv],
            device_id=to,
            device_id_type=pl.DeviceIdType.MESH,
        )

    def received(phase, ref, recv=0):
        remote(phase, ref, ref, sib, recv=recv).wait_recv()

    def sent(phase, ref, send=0):
        remote(phase, ref, ref, sib, send=send).wait_send()

    def local(i, src, dst):
        return pltpu.make_async_copy(src, dst, S["loc"][0].at[i])

    def cols(cc):
        return pl.ds(pl.multiple_of(cc * 128, 128), 128)

    def rows8(cc):
        return pl.ds(pl.multiple_of(cc * 8, 8), 8)

    def rows16(at):
        return pl.ds(pl.multiple_of(at * 16, 16), 16)

    def flush():
        for wait in pending:
            wait()
        pending.clear()

    loc = [
        local(0, g, B["gv"]),
        local(1, mom.at[:, :, cols(c)], B["mom16"].at[:, rows8(c), :]),
        local(2, mas.at[:, :, cols(c)], B["mas16"].at[:, rows8(c), :]),
        local(3, mas, B["mas"]),
    ]
    for item in loc:
        item.start()

    barrier = pltpu.get_barrier_semaphore()
    partners = [sib] + [xpeer(k) for k in range(1, NX)]
    partners += [ypeer(k) for k in range(1, NY)] + [zpeer(k) for k in range(1, NZ)]
    for to in partners:
        pl.semaphore_signal(barrier, inc=1, device_id=to, device_id_type=pl.DeviceIdType.MESH)
    pl.semaphore_wait(barrier, len(partners))
    ow_out[...] = jnp.zeros_like(ow_out)
    for item in loc:
        item.wait()
    yield "barrier", flush

    def each(order, op):
        for delta in order:
            m = (y + delta) % NY
            pl.when(m < NM)(functools.partial(op, m, delta))

    smo = remote("smo", mom.at[:, :, cols(oc)], B["mom16"].at[:, rows8(c), :], sib)
    sma = remote("sma", mas.at[:, :, cols(oc)], B["mas16"].at[:, rows8(c), :], sib)
    smo.start()
    sma.start()

    def swap(m, delta):
        remote("sg", B["gv"].at[m, :, cols(oc)], B["sib_g"].at[m], sib, recv=m).start()

    each(FAR, swap)
    pending += [lambda: sent("sg", B["sib_g"]), smo.wait_send, sma.wait_send]

    def pair(m, delta):
        received("sg", B["sib_g"].at[m], recv=m)

        def add(xx, carry):
            for yy in range(NY):
                rows = rows16(yy * 4 + xx)
                total = B["gv"][m, rows, cols(c)].astype(f32) + B["sib_g"][m, rows, :].astype(f32)
                B["sum1"][m, xx, pl.ds(yy * 16, 16), :] = total.astype(bf16)
            return carry

        lax.fori_loop(0, NX, add, 0)
        for k in (2, 1, 3):
            remote(
                "x1", B["sum1"].at[m, (x + k) % NX], B["xr"].at[m, k - 1], xpeer(k), recv=m
            ).start()

    each(FAR, pair)
    pending.append(lambda: sent("x1", B["xr"]))
    yield "pair", flush

    smo.wait_recv()
    sma.wait_recv()

    def my(m):
        slot = (m - y + NY) % NY - 1
        return remote("my", B["mom16"].at[m], B["momr"].at[y], dev(m, x, c, z), send=slot)

    def y1(m):
        slot = (m - y + NY) % NY - 1
        return remote("y1", B["sum2"].at[m], B["yr"].at[slot], dev(m, x, c, z), send=slot)

    def not_mine(op, m):
        @pl.when(y != m)
        def _():
            op(m)

    for m in range(NM):
        not_mine(lambda m: my(m).start(), m)

        @pl.when(y == m)
        def _(m=m):
            B["momr"][m] = B["mom16"][m]

    B["masb"][...] = B["mas16"][...].astype(bf16)
    for k in (4, 3, 5, 2, 6, 1, 7):
        remote("ay", B["masb"], B["mb"].at[c, x, y], ypeer(k)).start()
    B["mb"][c, x, y] = B["masb"][...]
    pending.append(lambda: sent("ay", B["mb"].at[c, x, pl.ds(0, NY - 1)]))

    def along_x(m, delta):
        received("x1", B["xr"].at[m], recv=m)
        total = B["sum1"][m, x].astype(f32)
        for k in range(1, NX):
            total = total + B["xr"][m, k - 1].astype(f32)
        B["sum2"][m] = total.astype(bf16)
        if delta:
            y1(m).start()

    each(FAR, along_x)
    for m in range(NM):
        pending.append(lambda m=m: not_mine(lambda m: my(m).wait_send(), m))
        pending.append(lambda m=m: not_mine(lambda m: y1(m).wait_send(), m))
    yield "x", flush

    def dot(left, right):
        return jnp.dot(left, right, preferred_element_type=f32)

    def ny(yy):
        return remote(
            "ny", B["nmw"].at[yy], B["nm16"].at[y], dev(yy, x, c, z), send=yy, recv=y
        )

    @pl.when(worker)
    def _():
        received("my", B["momr"].at[pl.ds(0, NY - 1)])
        received("y1", B["yr"])
        summed = B["sum2"][y].astype(f32)
        for k in range(1, NY):
            summed = summed + B["yr"][k - 1].astype(f32)
        new_mom = momentum_decay * B["momr"][...].reshape(128, 128) + summed
        B["u"][x] = (summed + momentum_decay * new_mom).astype(bf16)
        for k in (2, 1, 3):
            remote("ux", B["u"].at[x], B["u"].at[x], xpeer(k)).start()
        B["nmw"][...] = new_mom.reshape(NY, 16, 128)
        B["nm16"][y] = B["nmw"][y]
    yield "y", flush

    @pl.when(worker)
    def _():
        received("ux", B["u"].at[pl.ds(0, NX - 1)])
    yield "ux", flush

    @pl.when(worker)
    def _():
        B["part"][...] = lax.dot_general(
            B["u"][x], B["u"][...].reshape(KV, 128), (((1,), (1,)), ((), ())),
            preferred_element_type=f32,
        )
        B["gps"][...] = B["part"][pl.ds(pl.multiple_of(oc * 64, 64), 64), :].astype(bf16)
        gs = remote("gs", B["gps"], B["gpr"], sib)
        gs.start()
        gs.wait_recv()
        mine = B["part"][pl.ds(pl.multiple_of(c * 64, 64), 64), :] + B["gpr"][...].astype(f32)
        for p in range(NZ):
            at, to = (p // 2) * 16, (p % 2) * 256
            B["gzs"][p] = mine[at:at + 16, to:to + 256].astype(bf16)
        for k in (4, 3, 5, 2, 6, 1, 7):
            remote("zr", B["gzs"].at[(z + k) % NZ], B["gzr"].at[k - 1], zpeer(k)).start()
        for yy in range(NY):
            @pl.when(y != yy)
            def _(yy=yy):
                ny(yy).start()
    yield "gs", flush

    received("ay", B["mb"].at[c, x, pl.ds(0, NY - 1)])
    for k in range(1, NX):
        remote("ax", B["mb"].at[c, x], B["mb"].at[c, x], xpeer(k)).start()
    flush()
    pending.append(lambda: sent("ax", B["mb"].at[c, pl.ds(0, NX - 1)]))

    def drain_head():
        sent("ux", B["u"].at[pl.ds(0, NX - 1)])
        sent("gs", B["gps"])
        sent("zr", B["gzr"])
        for yy in range(NY):
            @pl.when(y != yy)
            def _(yy=yy):
                ny(yy).wait_send()

    pending.append(lambda: pl.when(worker)(drain_head))

    @pl.when(worker)
    def _():
        received("zr", B["gzr"])
        total = B["gzs"][z].astype(f32)
        for k in range(1, NZ):
            total = total + B["gzr"][k - 1].astype(f32)
        B["gz"][z] = total.astype(bf16)
        for k in (4, 3, 5, 2, 6, 1, 7):
            remote("za", B["gz"].at[z], B["gz"].at[z], zpeer(k)).start()
    pending.append(lambda: pl.when(worker)(lambda: sent("za", B["gz"].at[pl.ds(0, NZ - 1)])))
    yield "zr", flush

    @pl.when(worker)
    def _():
        received("za", B["gz"].at[pl.ds(0, NZ - 1)])
        for p in range(NZ):
            at, to = (p // 2) * 16, (p % 2) * 256
            B["g4"][c, x, at:at + 16, to:to + 256] = B["gz"][p]
        for k in (2, 1, 3):
            remote("gx", B["g4"].at[c, x], B["g4"].at[c, x], xpeer(k)).start()
    pending.append(lambda: pl.when(worker)(lambda: sent("gx", B["g4"].at[c, pl.ds(0, NX - 1)])))
    yield "za", flush

    @pl.when(worker)
    def _():
        received("gx", B["g4"].at[c, pl.ds(0, NX - 1)])
        gc = remote("gc", B["g4"].at[c], B["g4"].at[c], sib)
        gc.start()
        gc.wait_recv()
    pending.append(lambda: pl.when(worker)(lambda: sent("gc", B["g4"].at[c])))
    yield "gx", flush

    received("ax", B["mb"].at[c, pl.ds(0, NX - 1)])
    ac = remote("ac", B["mb"].at[c], B["mb"].at[c], sib)
    ac.start()
    pending.append(ac.wait_send)

    def sq(yy):
        return remote("sq", B["sqw"], B["sqr"].at[y], dev(yy, x, c, z), send=yy, recv=y)

    @pl.when(worker)
    def _():
        row = lax.broadcasted_iota(jnp.int32, (64, 128), 0)
        col = lax.broadcasted_iota(jnp.int32, (64, 128), 1)
        squares = jnp.zeros((64, 128), f32)
        for xx in range(NX):
            for cc in range(2):
                block = B["g4"][cc, xx, :, xx * 128:xx * 128 + 128].astype(f32)
                squares = squares + jnp.where(row + cc * 64 == col, block, 0.0)
        squares = jnp.sum(jnp.sum(squares, axis=0, keepdims=True), axis=1, keepdims=True)
        B["sqw"][...] = jnp.broadcast_to(squares, (8, 128))
        for yy in range(NY):
            @pl.when(y != yy)
            def _(yy=yy):
                sq(yy).start()
        B["sqr"][y] = B["sqw"][...]
        scale = 1.0 / (jnp.sqrt(squares) + epsilon)
        for xx in range(NX):
            for cc in range(2):
                at = (xx * 2 + cc) * 64
                B["gf"][at:at + 64, :] = (B["g4"][cc, xx].astype(f32) * scale) * scale
        gram = B["gf"][...]

        def mixing(gram, half):
            return (quintic_second * gram + quintic_third * dot(half, half)).astype(bf16)

        def advance(gram, half, mix):
            once = quintic_first * gram + dot(mix, half)
            return quintic_first * once + dot(once.astype(bf16), mix)

        B["gb"][...] = gram.astype(bf16)
        B["m0"][...] = mixing(gram, B["gb"][...])
        gram = advance(gram, B["gb"][...], B["m0"][...])
        B["gb"][...] = gram.astype(bf16)
        B["m1"][...] = mixing(gram, B["gb"][...])
        gram = advance(gram, B["gb"][...], B["m1"][...])
        B["gf"][...] = gram
        B["gb"][...] = gram.astype(bf16)
        mine = pl.ds(pl.multiple_of(x * 128, 128), 128)
        mix2 = (
            quintic_second * B["gf"][mine, :]
            + quintic_third * dot(B["gb"][mine, :], B["gb"][...])
        ).astype(bf16)
        k1 = quintic_first * (B["m1"][mine, :].astype(f32) + mix2.astype(f32)) + dot(
            mix2, B["m1"][...]
        )
        k0 = (
            quintic_first**2 * B["m0"][mine, :].astype(f32)
            + quintic_first * k1
            + dot(k1.astype(bf16), B["m0"][...])
        )
        last = quintic_first**3 * B["u"][x].astype(f32) + dot(
            k0.astype(bf16), B["u"][...].reshape(KV, 128)
        )
        last = (last * scale).astype(bf16)
        B["big"][c, y, x] = (factor * last.astype(f32)).astype(bf16)
    yield "ns", flush

    @pl.when(worker)
    def _():
        for k in NEAR[1:]:
            remote("sy", B["big"].at[c, y, x], B["big"].at[c, y, x], ypeer(k), recv=y).start()

    def drain_worker():
        sent("sy", B["yr"])
        for yy in range(NY):
            @pl.when(y != yy)
            def _(yy=yy):
                sq(yy).wait_send()

    for m in range(NM):
        not_mine(lambda m: received("ny", B["nm16"].at[m], recv=m), m)
    ns = remote("ns", B["nm16"].at[:, rows8(oc), :], B["nmsib"], sib)
    ns.start()
    pending.append(ns.wait_send)
    nm_out[:, :, cols(c)] = B["nm16"][:, rows8(c), :]
    ac.wait_recv()
    flush()
    ns.wait_recv()
    nm_out[:, :, cols(oc)] = B["nmsib"][...]

    def on_x(m, delta):
        if delta:
            received("sy", B["big"].at[c, m, x], recv=m)
        for k in (2, 1, 3):
            remote("sx", B["big"].at[c, m, x], B["big"].at[c, m, x], xpeer(k), recv=m).start()

    each(NEAR, on_x)
    pending.append(lambda: pl.when(worker)(drain_worker))
    pending.append(lambda: sent("sx", B["xr"]))
    yield "sy", flush

    def picks(m):
        mine = owners[m]
        slot = jnp.int32(0)
        for j in range(NM):
            slot = slot + ((owners[j] == mine) & (j < m)).astype(jnp.int32)
        return [(mine == d) & (slot == s) for s in range(MOST)]

    def finish(cc, m):
        chosen = picks(m)

        def one(xx, carry):
            for yy in range(NY):
                rows = rows16(yy * 4 + xx)
                scaled = B["big"][cc, m, xx, pl.ds(yy * 16, 16), :]
                master = B["mb"][cc, xx, yy, m].astype(f32)
                w_out[m, rows, cols(cc)] = (
                    master * (1.0 - learn_rate * weight_decay) - learn_rate * scaled.astype(f32)
                ).astype(bf16)
                for s in range(MOST):
                    ow_out[s, rows, cols(cc)] = jnp.where(
                        chosen[s], scaled, ow_out[s, rows, cols(cc)]
                    )
            return carry

        lax.fori_loop(0, NX, one, 0)
        own = B["big"][cc, m, x, pl.ds(pl.multiple_of(y * 16, 16), 16), :].astype(f32)
        own = jnp.where(c == 0, own[0:8], own[8:16])
        ma_out[m, :, cols(cc)] = (
            B["mas"][m, :, cols(cc)] * (1.0 - learn_rate * weight_decay) - learn_rate * own
        )

    for m in range(NM):
        not_mine(lambda m: received("sq", B["sqr"].at[m], recv=m), m)
    lane = lax.broadcasted_iota(jnp.int32, (1, 128), 1)
    rms = jnp.zeros((1, 128), f32)
    for m in range(NM):
        value = jnp.sqrt(B["sqr"][m, 0:1, :] / float(KV * D))
        chosen = picks(m)
        for s in range(MOST):
            rms = rms + jnp.where(chosen[s] & (lane == s), value, 0.0)
    rms_out[...] = rms[:, 0:MOST]

    def to_sibling(m, delta):
        received("sx", B["big"].at[c, m, pl.ds(0, NX - 1)], recv=m)
        remote("sc", B["big"].at[c, m], B["big"].at[c, m], sib, recv=m).start()

    def from_sibling(m, delta):
        received("sc", B["big"].at[oc, m], recv=m)
        finish(oc, m)

    for i, delta in enumerate(NEAR):
        each((delta,), to_sibling)
        if i:
            each((NEAR[i - 1],), from_sibling)
        each((delta,), lambda m, delta: finish(c, m))
    each((NEAR[-1],), from_sibling)
    pending.append(lambda: sent("sc", B["big"].at[c]))
    flush()


def kernel(stop, *refs):
    for name, flush in stages(*refs):
        if name == stop:
            flush()
            break


def step(owners, g, mom, mas, stop=None, collective_id=0):
    vmem = pl.BlockSpec(memory_space=pltpu.VMEM)
    hbm = pl.BlockSpec(memory_space=pltpu.HBM)
    scratch = [pltpu.VMEM(*spec) for spec in BUFFERS.values()]
    for send, recv in PHASES.values():
        scratch += [pltpu.SemaphoreType.DMA((send,)), pltpu.SemaphoreType.DMA((recv,))]
    return pl.pallas_call(
        functools.partial(kernel, stop),
        out_shape=(
            pltpu.VMEM((NM, KV, 256), bf16),
            pltpu.VMEM((NM, 8, 256), f32),
            pltpu.VMEM((NM, 8, 256), f32),
            pltpu.VMEM((MOST, KV, 256), bf16),
            pltpu.VMEM((1, MOST), f32),
        ),
        in_specs=[pl.BlockSpec(memory_space=pltpu.SMEM), hbm, hbm, hbm],
        out_specs=(vmem, vmem, vmem, vmem, vmem),
        scratch_shapes=scratch,
        compiler_params=pltpu.CompilerParams(
            collective_id=collective_id, has_side_effects=True, vmem_limit_bytes=40 * 1024 * 1024
        ),
        name="muon_step",
    )(*(pltpu.with_memory_space_constraint(item, pltpu.HBM) for item in (owners, g, mom, mas)))


def copy_kernel(*refs):
    count = (len(refs) - 1) // 2
    copies = [
        pltpu.make_async_copy(refs[i], refs[count + i], refs[-1].at[i]) for i in range(count)
    ]
    for copy in copies:
        copy.start()
    for copy in copies:
        copy.wait()


def write_out(arrays):
    return pl.pallas_call(
        copy_kernel,
        out_shape=[jax.ShapeDtypeStruct(item.shape, item.dtype) for item in arrays],
        in_specs=[pl.BlockSpec(memory_space=pl.ANY)] * len(arrays),
        out_specs=[pl.BlockSpec(memory_space=pl.ANY)] * len(arrays),
        scratch_shapes=[pltpu.SemaphoreType.DMA((len(arrays),))],
        name="write_out",
    )(*(pltpu.with_memory_space_constraint(item, pltpu.VMEM) for item in arrays))


def per_device(gradients, momentum, master, owners):
    new_weights, new_momentum, new_master, owned_updates, owned_rms = write_out(
        step(owners, gradients[0], momentum, master)
    )
    return (new_weights, new_master, new_momentum, owned_updates[None], owned_rms)


def solution(mesh):
    return jax.shard_map(
        per_device,
        mesh=mesh,
        in_specs=(P("dp", None, None, "col"), P(None, "dp", "col"), P(None, "dp", "col"), P()),
        out_specs=(
            P(None, None, "col"),
            P(None, "dp", "col"),
            P(None, "dp", "col"),
            P("dp", None, None, "col"),
            P("dp", None),
        ),
        check_vma=False,
    )
```

```python
import functools
import math

import jax
import jax.numpy as jnp
from jax import lax
from jax.experimental import pallas as pl
from jax.experimental.pallas import tpu as pltpu
from jax.sharding import PartitionSpec as P

KV = 512
D = 2048
NM = 6
MOST = 2
NY = 8
NX = 4
NZ = 8

quintic_first = 3.4445
quintic_second = -4.775
quintic_third = 2.0315
momentum_decay = 0.95
learn_rate = 0.3
weight_decay = 0.1
epsilon = 1e-07
factor = 0.2 * math.sqrt(max(KV, D))

f32 = jnp.float32
bf16 = jnp.bfloat16
FAR = (4, 3, 5, 2, 6, 1, 7, 0)
NEAR = (0, 1, 7, 2, 6, 3, 5, 4)

BUFFERS = dict(
    gv=((NM, KV, 256), bf16),
    sib_g=((NM, KV, 128), bf16),
    sum1=((NM, NX, 128, 128), bf16),
    xr=((NM, NX - 1, 128, 128), bf16),
    sum2=((NM, 128, 128), bf16),
    yr=((NY - 1, 128, 128), bf16),
    mas=((NM, 8, 256), f32),
    mom16=((NM, 16, 128), f32),
    mas16=((NM, 16, 128), f32),
    masb=((NM, 16, 128), bf16),
    momr=((NY, 16, 128), f32),
    nmw=((NY, 16, 128), f32),
    nm16=((NM, 16, 128), f32),
    nmsib=((NM, 8, 128), f32),
    u=((NX, 128, 128), bf16),
    part=((128, 512), f32),
    gps=((64, 512), bf16),
    gpr=((64, 512), bf16),
    gzs=((NZ, 16, 256), bf16),
    gzr=((NZ - 1, 16, 256), bf16),
    gz=((NZ, 16, 256), bf16),
    g4=((2, NX, 64, 512), bf16),
    gf=((512, 512), f32),
    gb=((512, 512), bf16),
    m0=((512, 512), bf16),
    m1=((512, 512), bf16),
    sqw=((8, 128), f32),
    sqr=((NM, 8, 128), f32),
    big=((2, NM, NX, 128, 128), bf16),
    mb=((2, NX, NY, NM, 16, 128), bf16),
)
PHASES = dict(
    loc=(5, 1), sg=(1, NM), smo=(1, 1), sma=(1, 1), x1=(1, NM), y1=(7, 1), my=(7, 1),
    ay=(1, 1), ux=(1, 1), gs=(1, 1), zr=(1, 1), za=(1, 1), gx=(1, 1), gc=(1, 1), ax=(2, 2),
    ac=(1, 1), ny=(8, NM), ns=(1, 1), sq=(8, NM), sy=(1, NM), sx=(1, NM), sc=(1, NM),
)


def stages(ids, g, mom, mas, w_out, nm_out, ma_out, ow_out, rms_out, owners, *scratch):
    names = list(BUFFERS)
    B = dict(zip(names, scratch[: len(names)]))
    sems = scratch[len(names):]
    S = {p: (sems[2 * i], sems[2 * i + 1]) for i, p in enumerate(PHASES)}
    pending = []

    d = lax.axis_index("dp")
    z = lax.axis_index("col")
    c = d % 2
    x = (d // 2) % NX
    y = d // 8
    oc = 1 - c
    worker = y < NM

    def dev(yy, xx, cc, zz):
        return ((yy * NX + xx) * 2 + cc, zz)

    sib = dev(y, x, oc, z)

    def xpeer(k):
        return dev(y, (x + k) % NX, c, z)

    def ypeer(k):
        return dev((y + k) % NY, x, c, z)

    def zpeer(k):
        return dev(y, x, c, (z + k) % NZ)

    def remote(phase, src, dst, to, send=0, recv=0):
        return pltpu.make_async_remote_copy(
            src_ref=src,
            dst_ref=dst,
            send_sem=S[phase][0].at[send],
            recv_sem=S[phase][1].at[recv],
            device_id=to,
            device_id_type=pl.DeviceIdType.MESH,
        )

    def received(phase, ref, recv=0):
        remote(phase, ref, ref, sib, recv=recv).wait_recv()

    def sent(phase, ref, send=0):
        remote(phase, ref, ref, sib, send=send).wait_send()

    def local(i, src, dst):
        return pltpu.make_async_copy(src, dst, S["loc"][0].at[i])

    def cols(cc):
        return pl.ds(pl.multiple_of(cc * 128, 128), 128)

    def rows8(cc):
        return pl.ds(pl.multiple_of(cc * 8, 8), 8)

    def rows16(at):
        return pl.ds(pl.multiple_of(at * 16, 16), 16)

    def flush():
        for wait in pending:
            wait()
        pending.clear()

    barrier = pltpu.get_barrier_semaphore()
    partners = [step(k) for k in (4, 3, 5, 2, 6, 1, 7) for step in (zpeer, ypeer)]
    partners += [xpeer(k) for k in (2, 1, 3)] + [sib]
    for to in partners:
        pl.semaphore_signal(barrier, inc=1, device_id=to, device_id_type=pl.DeviceIdType.MESH)
    loc = [
        local(0, g, B["gv"]),
        local(1, mom.at[:, :, cols(c)], B["mom16"].at[:, rows8(c), :]),
        local(2, mas.at[:, :, cols(c)], B["mas16"].at[:, rows8(c), :]),
        local(3, mas, B["mas"]),
        local(4, ids, owners),
    ]
    for item in loc:
        item.start()
    ow_out[...] = jnp.zeros_like(ow_out)
    loc[0].wait()
    pl.semaphore_wait(barrier, len(partners))
    yield "barrier", flush

    def each(order, op):
        for delta in order:
            m = (y + delta) % NY
            pl.when(m < NM)(functools.partial(op, m, delta))

    smo = remote("smo", mom.at[:, :, cols(oc)], B["mom16"].at[:, rows8(c), :], sib)
    sma = remote("sma", mas.at[:, :, cols(oc)], B["mas16"].at[:, rows8(c), :], sib)
    smo.start()
    sma.start()

    def swap(m, delta):
        remote("sg", B["gv"].at[m, :, cols(oc)], B["sib_g"].at[m], sib, recv=m).start()

    each(FAR, swap)
    for item in loc[1:]:
        item.wait()
    pending += [lambda: sent("sg", B["sib_g"]), smo.wait_send, sma.wait_send]

    def pair(m, delta):
        received("sg", B["sib_g"].at[m], recv=m)

        def add(xx, carry):
            for yy in range(NY):
                rows = rows16(yy * 4 + xx)
                total = B["gv"][m, rows, cols(c)].astype(f32) + B["sib_g"][m, rows, :].astype(f32)
                B["sum1"][m, xx, pl.ds(yy * 16, 16), :] = total.astype(bf16)
            return carry

        lax.fori_loop(0, NX, add, 0)
        for k in (2, 1, 3):
            remote(
                "x1", B["sum1"].at[m, (x + k) % NX], B["xr"].at[m, k - 1], xpeer(k), recv=m
            ).start()

    each(FAR, pair)
    pending.append(lambda: sent("x1", B["xr"]))
    yield "pair", flush

    smo.wait_recv()
    sma.wait_recv()

    def my(m):
        slot = (m - y + NY) % NY - 1
        return remote("my", B["mom16"].at[m], B["momr"].at[y], dev(m, x, c, z), send=slot)

    def y1(m):
        slot = (m - y + NY) % NY - 1
        return remote("y1", B["sum2"].at[m], B["yr"].at[slot], dev(m, x, c, z), send=slot)

    def not_mine(op, m):
        @pl.when(y != m)
        def _():
            op(m)

    for m in range(NM):
        not_mine(lambda m: my(m).start(), m)

        @pl.when(y == m)
        def _(m=m):
            B["momr"][m] = B["mom16"][m]

    B["masb"][...] = B["mas16"][...].astype(bf16)
    for k in (4, 3, 5, 2, 6, 1, 7):
        remote("ay", B["masb"], B["mb"].at[c, x, y], ypeer(k)).start()
    B["mb"][c, x, y] = B["masb"][...]
    pending.append(lambda: sent("ay", B["mb"].at[c, x, pl.ds(0, NY - 1)]))

    def along_x(m, delta):
        received("x1", B["xr"].at[m], recv=m)
        total = B["sum1"][m, x].astype(f32)
        for k in range(1, NX):
            total = total + B["xr"][m, k - 1].astype(f32)
        B["sum2"][m] = total.astype(bf16)
        if delta:
            y1(m).start()

    each(FAR, along_x)
    for m in range(NM):
        pending.append(lambda m=m: not_mine(lambda m: my(m).wait_send(), m))
        pending.append(lambda m=m: not_mine(lambda m: y1(m).wait_send(), m))
    yield "x", flush

    def dot(left, right):
        return jnp.dot(left, right, preferred_element_type=f32)

    def ny(yy):
        return remote(
            "ny", B["nmw"].at[yy], B["nm16"].at[y], dev(yy, x, c, z), send=yy, recv=y
        )

    @pl.when(worker)
    def _():
        received("my", B["momr"].at[pl.ds(0, NY - 1)])
        received("y1", B["yr"])
        summed = B["sum2"][y].astype(f32)
        for k in range(1, NY):
            summed = summed + B["yr"][k - 1].astype(f32)
        new_mom = momentum_decay * B["momr"][...].reshape(128, 128) + summed
        B["u"][x] = (summed + momentum_decay * new_mom).astype(bf16)
        for k in (2, 1, 3):
            remote("ux", B["u"].at[x], B["u"].at[x], xpeer(k)).start()
        B["nmw"][...] = new_mom.reshape(NY, 16, 128)
        B["nm16"][y] = B["nmw"][y]
    yield "y", flush

    @pl.when(worker)
    def _():
        received("ux", B["u"].at[pl.ds(0, NX - 1)])
    yield "ux", flush

    @pl.when(worker)
    def _():
        B["part"][...] = lax.dot_general(
            B["u"][x], B["u"][...].reshape(KV, 128), (((1,), (1,)), ((), ())),
            preferred_element_type=f32,
        )
        B["gps"][...] = B["part"][pl.ds(pl.multiple_of(oc * 64, 64), 64), :].astype(bf16)
        gs = remote("gs", B["gps"], B["gpr"], sib)
        gs.start()
        gs.wait_recv()
        mine = B["part"][pl.ds(pl.multiple_of(c * 64, 64), 64), :] + B["gpr"][...].astype(f32)
        for p in range(NZ):
            at, to = (p // 2) * 16, (p % 2) * 256
            B["gzs"][p] = mine[at:at + 16, to:to + 256].astype(bf16)
        for k in (4, 3, 5, 2, 6, 1, 7):
            remote("zr", B["gzs"].at[(z + k) % NZ], B["gzr"].at[k - 1], zpeer(k)).start()
        for yy in range(NY):
            @pl.when(y != yy)
            def _(yy=yy):
                ny(yy).start()
    yield "gs", flush

    received("ay", B["mb"].at[c, x, pl.ds(0, NY - 1)])
    def ax(k, part):
        return remote(
            "ax", B["mb"].at[c, x], B["mb"].at[c, x], xpeer(k), send=part, recv=part
        )

    ax(1, 0).start()
    ax(3, 0).start()
    flush()
    pending.append(lambda: sent("ax", B["mb"].at[c, pl.ds(0, 2)], send=0))

    def drain_head():
        sent("ux", B["u"].at[pl.ds(0, NX - 1)])
        sent("gs", B["gps"])
        sent("zr", B["gzr"])
        for yy in range(NY):
            @pl.when(y != yy)
            def _(yy=yy):
                ny(yy).wait_send()

    pending.append(lambda: pl.when(worker)(drain_head))

    @pl.when(worker)
    def _():
        received("zr", B["gzr"])
        total = B["gzs"][z].astype(f32)
        for k in range(1, NZ):
            total = total + B["gzr"][k - 1].astype(f32)
        B["gz"][z] = total.astype(bf16)
        for k in (4, 3, 5, 2, 6, 1, 7):
            remote("za", B["gz"].at[z], B["gz"].at[z], zpeer(k)).start()

    ax(2, 1).start()
    pending.append(ax(2, 1).wait_send)

    pending.append(lambda: pl.when(worker)(lambda: sent("za", B["gz"].at[pl.ds(0, NZ - 1)])))
    yield "zr", flush

    @pl.when(worker)
    def _():
        received("za", B["gz"].at[pl.ds(0, NZ - 1)])
        for p in range(NZ):
            at, to = (p // 2) * 16, (p % 2) * 256
            B["g4"][c, x, at:at + 16, to:to + 256] = B["gz"][p]
        for k in (2, 1, 3):
            remote("gx", B["g4"].at[c, x], B["g4"].at[c, x], xpeer(k)).start()
    pending.append(lambda: pl.when(worker)(lambda: sent("gx", B["g4"].at[c, pl.ds(0, NX - 1)])))
    yield "za", flush

    @pl.when(worker)
    def _():
        received("gx", B["g4"].at[c, pl.ds(0, NX - 1)])
        gc = remote("gc", B["g4"].at[c], B["g4"].at[c], sib)
        gc.start()
        gc.wait_recv()
    pending.append(lambda: pl.when(worker)(lambda: sent("gc", B["g4"].at[c])))
    yield "gx", flush

    received("ax", B["mb"].at[c, pl.ds(0, 2)], recv=0)
    received("ax", B["mb"].at[c, x], recv=1)
    ac = remote("ac", B["mb"].at[c], B["mb"].at[c], sib)
    ac.start()
    pending.append(ac.wait_send)

    def sq(yy):
        return remote("sq", B["sqw"], B["sqr"].at[y], dev(yy, x, c, z), send=yy, recv=y)

    @pl.when(worker)
    def _():
        row = lax.broadcasted_iota(jnp.int32, (64, 128), 0)
        col = lax.broadcasted_iota(jnp.int32, (64, 128), 1)
        squares = jnp.zeros((64, 128), f32)
        for xx in range(NX):
            for cc in range(2):
                block = B["g4"][cc, xx, :, xx * 128:xx * 128 + 128].astype(f32)
                squares = squares + jnp.where(row + cc * 64 == col, block, 0.0)
        squares = jnp.sum(jnp.sum(squares, axis=0, keepdims=True), axis=1, keepdims=True)
        B["sqw"][...] = jnp.broadcast_to(squares, (8, 128))
        for yy in range(NY):
            @pl.when(y != yy)
            def _(yy=yy):
                sq(yy).start()
        B["sqr"][y] = B["sqw"][...]
        scale = 1.0 / (jnp.sqrt(squares) + epsilon)
        for xx in range(NX):
            for cc in range(2):
                at = (xx * 2 + cc) * 64
                B["gf"][at:at + 64, :] = (B["g4"][cc, xx].astype(f32) * scale) * scale
        gram = B["gf"][...]

        def mixing(gram, half):
            return (quintic_second * gram + quintic_third * dot(half, half)).astype(bf16)

        def advance(gram, half, mix):
            once = quintic_first * gram + dot(mix, half)
            return quintic_first * once + dot(once.astype(bf16), mix)

        B["gb"][...] = gram.astype(bf16)
        B["m0"][...] = mixing(gram, B["gb"][...])
        gram = advance(gram, B["gb"][...], B["m0"][...])
        B["gb"][...] = gram.astype(bf16)
        B["m1"][...] = mixing(gram, B["gb"][...])
        gram = advance(gram, B["gb"][...], B["m1"][...])
        B["gf"][...] = gram
        B["gb"][...] = gram.astype(bf16)
        mine = pl.ds(pl.multiple_of(x * 128, 128), 128)
        mix2 = (
            quintic_second * B["gf"][mine, :]
            + quintic_third * dot(B["gb"][mine, :], B["gb"][...])
        ).astype(bf16)
        k1 = quintic_first * (B["m1"][mine, :].astype(f32) + mix2.astype(f32)) + dot(
            mix2, B["m1"][...]
        )
        k0 = (
            quintic_first**2 * B["m0"][mine, :].astype(f32)
            + quintic_first * k1
            + dot(k1.astype(bf16), B["m0"][...])
        )
        last = quintic_first**3 * B["u"][x].astype(f32) + dot(
            k0.astype(bf16), B["u"][...].reshape(KV, 128)
        )
        last = (last * scale).astype(bf16)
        B["big"][c, y, x] = (factor * last.astype(f32)).astype(bf16)
    yield "ns", flush

    def sy(k):
        return remote("sy", B["big"].at[c, y, x], B["big"].at[c, y, x], ypeer(k), recv=y)

    def sx(m):
        for k in (2, 1, 3):
            remote("sx", B["big"].at[c, m, x], B["big"].at[c, m, x], xpeer(k), recv=m).start()

    @pl.when(worker)
    def _():
        sy(1).start()
        sy(7).start()
        sx(y)
        sy(2).start()
        sy(6).start()

    def drain_worker():
        sent("sy", B["yr"])
        for yy in range(NY):
            @pl.when(y != yy)
            def _(yy=yy):
                sq(yy).wait_send()

    for m in range(NM):
        not_mine(lambda m: received("ny", B["nm16"].at[m], recv=m), m)
    ns = remote("ns", B["nm16"].at[:, rows8(oc), :], B["nmsib"], sib)
    ns.start()
    pending.append(ns.wait_send)
    nm_out[:, :, cols(c)] = B["nm16"][:, rows8(c), :]
    ac.wait_recv()
    flush()
    ns.wait_recv()
    nm_out[:, :, cols(oc)] = B["nmsib"][...]

    def picks(m):
        mine = owners[m]
        slot = jnp.int32(0)
        for j in range(NM):
            slot = slot + ((owners[j] == mine) & (j < m)).astype(jnp.int32)
        return [(mine == d) & (slot == s) for s in range(MOST)]

    for m in range(NM):
        not_mine(lambda m: received("sq", B["sqr"].at[m], recv=m), m)
    lane = lax.broadcasted_iota(jnp.int32, (1, 128), 1)
    rms = jnp.zeros((1, 128), f32)
    for m in range(NM):
        value = jnp.sqrt(B["sqr"][m, 0:1, :] / float(KV * D))
        chosen = picks(m)
        for s in range(MOST):
            rms = rms + jnp.where(chosen[s] & (lane == s), value, 0.0)
    rms_out[...] = rms[:, 0:MOST]

    @pl.when(worker)
    def _():
        for k in (3, 5, 4):
            sy(k).start()

    def on_x(m, delta):
        received("sy", B["big"].at[c, m, x], recv=m)
        sx(m)

    each(NEAR[1:], on_x)
    pending.append(lambda: pl.when(worker)(drain_worker))
    pending.append(lambda: sent("sx", B["xr"]))
    yield "sy", flush

    def finish(cc, m):
        chosen = picks(m)

        def one(xx, carry):
            for yy in range(NY):
                rows = rows16(yy * 4 + xx)
                scaled = B["big"][cc, m, xx, pl.ds(yy * 16, 16), :]
                master = B["mb"][cc, xx, yy, m].astype(f32)
                w_out[m, rows, cols(cc)] = (
                    master * (1.0 - learn_rate * weight_decay) - learn_rate * scaled.astype(f32)
                ).astype(bf16)
                for s in range(MOST):
                    ow_out[s, rows, cols(cc)] = jnp.where(
                        chosen[s], scaled, ow_out[s, rows, cols(cc)]
                    )
            return carry

        lax.fori_loop(0, NX, one, 0)
        own = B["big"][cc, m, x, pl.ds(pl.multiple_of(y * 16, 16), 16), :].astype(f32)
        own = jnp.where(c == 0, own[0:8], own[8:16])
        ma_out[m, :, cols(cc)] = (
            B["mas"][m, :, cols(cc)] * (1.0 - learn_rate * weight_decay) - learn_rate * own
        )

    def to_sibling(m, delta):
        received("sx", B["big"].at[c, m, pl.ds(0, NX - 1)], recv=m)
        remote("sc", B["big"].at[c, m], B["big"].at[c, m], sib, recv=m).start()

    def from_sibling(m, delta):
        received("sc", B["big"].at[oc, m], recv=m)
        finish(oc, m)

    for i, delta in enumerate(NEAR):
        each((delta,), to_sibling)
        if i:
            each((NEAR[i - 1],), from_sibling)
        each((delta,), lambda m, delta: finish(c, m))
    each((NEAR[-1],), from_sibling)
    pending.append(lambda: sent("sc", B["big"].at[c]))
    flush()


def kernel(stop, *refs):
    for name, flush in stages(*refs):
        if name == stop:
            flush()
            break


def step(owners, g, mom, mas, stop=None, collective_id=0):
    vmem = pl.BlockSpec(memory_space=pltpu.VMEM)
    hbm = pl.BlockSpec(memory_space=pltpu.HBM)
    scratch = [pltpu.SMEM((NM,), jnp.int32)]
    scratch += [pltpu.VMEM(*spec) for spec in BUFFERS.values()]
    for send, recv in PHASES.values():
        scratch += [pltpu.SemaphoreType.DMA((send,)), pltpu.SemaphoreType.DMA((recv,))]
    return pl.pallas_call(
        functools.partial(kernel, stop),
        out_shape=(
            pltpu.VMEM((NM, KV, 256), bf16),
            pltpu.VMEM((NM, 8, 256), f32),
            pltpu.VMEM((NM, 8, 256), f32),
            pltpu.VMEM((MOST, KV, 256), bf16),
            pltpu.VMEM((1, MOST), f32),
        ),
        in_specs=[hbm, hbm, hbm, hbm],
        out_specs=(vmem, vmem, vmem, vmem, vmem),
        scratch_shapes=scratch,
        compiler_params=pltpu.CompilerParams(
            collective_id=collective_id, has_side_effects=True, vmem_limit_bytes=40 * 1024 * 1024
        ),
        name="muon_step",
    )(*(pltpu.with_memory_space_constraint(item, pltpu.HBM) for item in (owners, g, mom, mas)))


def copy_kernel(*refs):
    count = (len(refs) - 1) // 2
    copies = [
        pltpu.make_async_copy(refs[i], refs[count + i], refs[-1].at[i]) for i in range(count)
    ]
    for copy in copies:
        copy.start()
    for copy in copies:
        copy.wait()


def write_out(arrays):
    return pl.pallas_call(
        copy_kernel,
        out_shape=[jax.ShapeDtypeStruct(item.shape, item.dtype) for item in arrays],
        in_specs=[pl.BlockSpec(memory_space=pl.ANY)] * len(arrays),
        out_specs=[pl.BlockSpec(memory_space=pl.ANY)] * len(arrays),
        scratch_shapes=[pltpu.SemaphoreType.DMA((len(arrays),))],
        name="write_out",
    )(*(pltpu.with_memory_space_constraint(item, pltpu.VMEM) for item in arrays))


def per_device(gradients, momentum, master, owners):
    new_weights, new_momentum, new_master, owned_updates, owned_rms = write_out(
        step(owners, gradients[0], momentum, master)
    )
    return (new_weights, new_master, new_momentum, owned_updates[None], owned_rms)


def solution(mesh):
    return jax.shard_map(
        per_device,
        mesh=mesh,
        in_specs=(P("dp", None, None, "col"), P(None, "dp", "col"), P(None, "dp", "col"), P()),
        out_specs=(
            P(None, None, "col"),
            P(None, "dp", "col"),
            P(None, "dp", "col"),
            P("dp", None, None, "col"),
            P("dp", None),
        ),
        check_vma=False,
    )
```

```python
import functools
import math

import jax
import jax.numpy as jnp
from jax import lax
from jax.experimental import pallas as pl
from jax.experimental.pallas import tpu as pltpu
from jax.sharding import PartitionSpec as P

KV = 512
D = 2048
NM = 6
MOST = 2
NY = 8
NX = 4
NZ = 8

quintic_first = 3.4445
quintic_second = -4.775
quintic_third = 2.0315
momentum_decay = 0.95
learn_rate = 0.3
weight_decay = 0.1
epsilon = 1e-07
factor = 0.2 * math.sqrt(max(KV, D))

f32 = jnp.float32
bf16 = jnp.bfloat16
FAR = (4, 3, 5, 2, 6, 1, 7, 0)
NEAR = (0, 1, 7, 2, 6, 3, 5, 4)

BUFFERS = dict(
    gv=((NM, KV, 256), bf16),
    sib_g=((NM, KV, 128), bf16),
    sum1=((NM, NX, 128, 128), bf16),
    xr=((NM, NX - 1, 128, 128), bf16),
    sum2=((NM, 128, 128), bf16),
    yr=((NY - 1, 128, 128), bf16),
    mas=((NM, 8, 256), f32),
    mom16=((NM, 16, 128), f32),
    mas16=((NM, 16, 128), f32),
    masb=((NM, 16, 128), bf16),
    momr=((NY, 16, 128), f32),
    nmw=((NY, 16, 128), f32),
    nm16=((NM, 16, 128), f32),
    nmsib=((NM, 8, 128), f32),
    u=((NX, 128, 128), bf16),
    part=((128, 512), f32),
    gps=((64, 512), bf16),
    gpr=((64, 512), bf16),
    gzs=((NZ, 16, 256), bf16),
    gzr=((NZ - 1, 16, 256), bf16),
    gz=((NZ, 16, 256), bf16),
    g4=((2, NX, 64, 512), bf16),
    gf=((512, 512), f32),
    gb=((512, 512), bf16),
    m0=((512, 512), bf16),
    m1=((512, 512), bf16),
    sqw=((8, 128), f32),
    sqr=((NM, 8, 128), f32),
    big=((2, NM, NX, 128, 128), bf16),
    mb=((2, NX, NY, NM, 16, 128), bf16),
)
PHASES = dict(
    loc=(5, 1), sg=(1, NM), smo=(1, 1), sma=(1, 1), x1=(1, NM), y1=(7, 1), my=(7, 1),
    ay=(1, 1), ux=(1, 1), gs=(1, 1), zr=(1, 1), za=(1, 1), gx=(1, NX - 1), gc=(1, 1), ax=(2, 2),
    ac=(1, 1), ny=(8, NM), ns=(1, 1), sq=(8, NM), sy=(1, NM), sx=(1, NM), sc=(1, NM),
)


def stages(ids, g, mom, mas, w_out, nm_out, ma_out, ow_out, rms_out, owners, *scratch):
    names = list(BUFFERS)
    B = dict(zip(names, scratch[: len(names)]))
    sems = scratch[len(names):]
    S = {p: (sems[2 * i], sems[2 * i + 1]) for i, p in enumerate(PHASES)}
    pending = []

    d = lax.axis_index("dp")
    z = lax.axis_index("col")
    c = d % 2
    x = (d // 2) % NX
    y = d // 8
    oc = 1 - c
    worker = y < NM

    def dev(yy, xx, cc, zz):
        return ((yy * NX + xx) * 2 + cc, zz)

    sib = dev(y, x, oc, z)

    def xpeer(k):
        return dev(y, (x + k) % NX, c, z)

    def ypeer(k):
        return dev((y + k) % NY, x, c, z)

    def zpeer(k):
        return dev(y, x, c, (z + k) % NZ)

    def remote(phase, src, dst, to, send=0, recv=0):
        return pltpu.make_async_remote_copy(
            src_ref=src,
            dst_ref=dst,
            send_sem=S[phase][0].at[send],
            recv_sem=S[phase][1].at[recv],
            device_id=to,
            device_id_type=pl.DeviceIdType.MESH,
        )

    def received(phase, ref, recv=0):
        remote(phase, ref, ref, sib, recv=recv).wait_recv()

    def sent(phase, ref, send=0):
        remote(phase, ref, ref, sib, send=send).wait_send()

    def local(i, src, dst):
        return pltpu.make_async_copy(src, dst, S["loc"][0].at[i])

    def cols(cc):
        return pl.ds(pl.multiple_of(cc * 128, 128), 128)

    def rows8(cc):
        return pl.ds(pl.multiple_of(cc * 8, 8), 8)

    def rows16(at):
        return pl.ds(pl.multiple_of(at * 16, 16), 16)

    def flush():
        for wait in pending:
            wait()
        pending.clear()

    barrier = pltpu.get_barrier_semaphore()
    partners = [step(k) for k in (4, 3, 5, 2, 6, 1, 7) for step in (zpeer, ypeer)]
    partners += [xpeer(k) for k in (2, 1, 3)] + [sib]
    for to in partners:
        pl.semaphore_signal(barrier, inc=1, device_id=to, device_id_type=pl.DeviceIdType.MESH)
    loc = [
        local(0, g, B["gv"]),
        local(1, mom.at[:, :, cols(c)], B["mom16"].at[:, rows8(c), :]),
        local(2, mas.at[:, :, cols(c)], B["mas16"].at[:, rows8(c), :]),
        local(3, mas, B["mas"]),
        local(4, ids, owners),
    ]
    for item in loc:
        item.start()
    ow_out[...] = jnp.zeros_like(ow_out)
    loc[0].wait()
    pl.semaphore_wait(barrier, len(partners))
    yield "barrier", flush

    def each(order, op):
        for delta in order:
            m = (y + delta) % NY
            pl.when(m < NM)(functools.partial(op, m, delta))

    smo = remote("smo", mom.at[:, :, cols(oc)], B["mom16"].at[:, rows8(c), :], sib)
    sma = remote("sma", mas.at[:, :, cols(oc)], B["mas16"].at[:, rows8(c), :], sib)
    smo.start()
    sma.start()

    def swap(m, delta):
        remote("sg", B["gv"].at[m, :, cols(oc)], B["sib_g"].at[m], sib, recv=m).start()

    each(FAR, swap)
    for item in loc[1:]:
        item.wait()
    pending += [lambda: sent("sg", B["sib_g"]), smo.wait_send, sma.wait_send]

    def pair(m, delta):
        received("sg", B["sib_g"].at[m], recv=m)

        def add(xx, carry):
            for yy in range(NY):
                rows = rows16(yy * 4 + xx)
                total = B["gv"][m, rows, cols(c)].astype(f32) + B["sib_g"][m, rows, :].astype(f32)
                B["sum1"][m, xx, pl.ds(yy * 16, 16), :] = total.astype(bf16)
            return carry

        lax.fori_loop(0, NX, add, 0)
        for k in (2, 1, 3):
            remote(
                "x1", B["sum1"].at[m, (x + k) % NX], B["xr"].at[m, k - 1], xpeer(k), recv=m
            ).start()

    each(FAR, pair)
    pending.append(lambda: sent("x1", B["xr"]))
    yield "pair", flush

    smo.wait_recv()
    sma.wait_recv()

    def my(m):
        slot = (m - y + NY) % NY - 1
        return remote("my", B["mom16"].at[m], B["momr"].at[y], dev(m, x, c, z), send=slot)

    def y1(m):
        slot = (m - y + NY) % NY - 1
        return remote("y1", B["sum2"].at[m], B["yr"].at[slot], dev(m, x, c, z), send=slot)

    def not_mine(op, m):
        @pl.when(y != m)
        def _():
            op(m)

    for m in range(NM):
        not_mine(lambda m: my(m).start(), m)

        @pl.when(y == m)
        def _(m=m):
            B["momr"][m] = B["mom16"][m]

    B["masb"][...] = B["mas16"][...].astype(bf16)
    for k in (4, 3, 5, 2, 6, 1, 7):
        remote("ay", B["masb"], B["mb"].at[c, x, y], ypeer(k)).start()
    B["mb"][c, x, y] = B["masb"][...]
    pending.append(lambda: sent("ay", B["mb"].at[c, x, pl.ds(0, NY - 1)]))

    def along_x(m, delta):
        received("x1", B["xr"].at[m], recv=m)
        total = B["sum1"][m, x].astype(f32)
        for k in range(1, NX):
            total = total + B["xr"][m, k - 1].astype(f32)
        B["sum2"][m] = total.astype(bf16)
        if delta:
            y1(m).start()

    each(FAR, along_x)
    for m in range(NM):
        pending.append(lambda m=m: not_mine(lambda m: my(m).wait_send(), m))
        pending.append(lambda m=m: not_mine(lambda m: y1(m).wait_send(), m))
    yield "x", flush

    def dot(left, right):
        return jnp.dot(left, right, preferred_element_type=f32)

    def ny(yy):
        return remote(
            "ny", B["nmw"].at[yy], B["nm16"].at[y], dev(yy, x, c, z), send=yy, recv=y
        )

    @pl.when(worker)
    def _():
        received("my", B["momr"].at[pl.ds(0, NY - 1)])
        received("y1", B["yr"])
        summed = B["sum2"][y].astype(f32)
        for k in range(1, NY):
            summed = summed + B["yr"][k - 1].astype(f32)
        new_mom = momentum_decay * B["momr"][...].reshape(128, 128) + summed
        B["u"][x] = (summed + momentum_decay * new_mom).astype(bf16)
        for k in (2, 1, 3):
            remote("ux", B["u"].at[x], B["u"].at[x], xpeer(k)).start()
        B["nmw"][...] = new_mom.reshape(NY, 16, 128)
        B["nm16"][y] = B["nmw"][y]
    yield "y", flush

    @pl.when(worker)
    def _():
        received("ux", B["u"].at[pl.ds(0, NX - 1)])
    yield "ux", flush

    @pl.when(worker)
    def _():
        B["part"][...] = lax.dot_general(
            B["u"][x], B["u"][...].reshape(KV, 128), (((1,), (1,)), ((), ())),
            preferred_element_type=f32,
        )
        B["gps"][...] = B["part"][pl.ds(pl.multiple_of(oc * 64, 64), 64), :].astype(bf16)
        gs = remote("gs", B["gps"], B["gpr"], sib)
        gs.start()
        gs.wait_recv()
        mine = B["part"][pl.ds(pl.multiple_of(c * 64, 64), 64), :] + B["gpr"][...].astype(f32)
        for p in range(NZ):
            at, to = (p // 2) * 16, (p % 2) * 256
            B["gzs"][p] = mine[at:at + 16, to:to + 256].astype(bf16)
        for k in (4, 3, 5, 2, 6, 1, 7):
            remote("zr", B["gzs"].at[(z + k) % NZ], B["gzr"].at[k - 1], zpeer(k)).start()
        for yy in range(NY):
            @pl.when(y != yy)
            def _(yy=yy):
                ny(yy).start()
    yield "gs", flush

    received("ay", B["mb"].at[c, x, pl.ds(0, NY - 1)])
    def ax(k, part):
        return remote(
            "ax", B["mb"].at[c, x], B["mb"].at[c, x], xpeer(k), send=part, recv=part
        )

    ax(1, 0).start()
    ax(3, 0).start()
    flush()
    pending.append(lambda: sent("ax", B["mb"].at[c, pl.ds(0, 2)], send=0))

    def drain_head():
        sent("ux", B["u"].at[pl.ds(0, NX - 1)])
        sent("gs", B["gps"])
        sent("zr", B["gzr"])
        for yy in range(NY):
            @pl.when(y != yy)
            def _(yy=yy):
                ny(yy).wait_send()

    pending.append(lambda: pl.when(worker)(drain_head))

    @pl.when(worker)
    def _():
        received("zr", B["gzr"])
        total = B["gzs"][z].astype(f32)
        for k in range(1, NZ):
            total = total + B["gzr"][k - 1].astype(f32)
        B["gz"][z] = total.astype(bf16)
        for k in (4, 3, 5, 2, 6, 1, 7):
            remote("za", B["gz"].at[z], B["gz"].at[z], zpeer(k)).start()

    ax(2, 1).start()
    pending.append(ax(2, 1).wait_send)

    pending.append(lambda: pl.when(worker)(lambda: sent("za", B["gz"].at[pl.ds(0, NZ - 1)])))
    yield "zr", flush

    def gc(k):
        part = B["g4"].at[c, (x + NX - k) % NX]
        return remote("gc", part, part, sib)

    @pl.when(worker)
    def _():
        received("za", B["gz"].at[pl.ds(0, NZ - 1)])
        for p in range(NZ):
            at, to = (p // 2) * 16, (p % 2) * 256
            B["g4"][c, x, at:at + 16, to:to + 256] = B["gz"][p]
        for k in (2, 1, 3):
            remote("gx", B["g4"].at[c, x], B["g4"].at[c, x], xpeer(k), recv=k - 1).start()
        gc(0).start()
    pending.append(lambda: pl.when(worker)(lambda: sent("gx", B["g4"].at[c, pl.ds(0, NX - 1)])))
    yield "za", flush

    @pl.when(worker)
    def _():
        for k in (1, 3, 2):
            received("gx", B["g4"].at[c, (x + NX - k) % NX], recv=k - 1)
            gc(k).start()
        received("gc", B["g4"].at[oc])
    pending.append(lambda: pl.when(worker)(lambda: sent("gc", B["g4"].at[c])))
    yield "gx", flush

    received("ax", B["mb"].at[c, pl.ds(0, 2)], recv=0)
    received("ax", B["mb"].at[c, x], recv=1)
    ac = remote("ac", B["mb"].at[c], B["mb"].at[c], sib)
    ac.start()
    pending.append(ac.wait_send)

    def sq(yy):
        return remote("sq", B["sqw"], B["sqr"].at[y], dev(yy, x, c, z), send=yy, recv=y)

    @pl.when(worker)
    def _():
        row = lax.broadcasted_iota(jnp.int32, (64, 128), 0)
        col = lax.broadcasted_iota(jnp.int32, (64, 128), 1)
        squares = jnp.zeros((64, 128), f32)
        for xx in range(NX):
            for cc in range(2):
                block = B["g4"][cc, xx, :, xx * 128:xx * 128 + 128].astype(f32)
                squares = squares + jnp.where(row + cc * 64 == col, block, 0.0)
        squares = jnp.sum(jnp.sum(squares, axis=0, keepdims=True), axis=1, keepdims=True)
        B["sqw"][...] = jnp.broadcast_to(squares, (8, 128))
        for yy in range(NY):
            @pl.when(y != yy)
            def _(yy=yy):
                sq(yy).start()
        B["sqr"][y] = B["sqw"][...]
        scale = 1.0 / (jnp.sqrt(squares) + epsilon)
        for xx in range(NX):
            for cc in range(2):
                at = (xx * 2 + cc) * 64
                B["gf"][at:at + 64, :] = (B["g4"][cc, xx].astype(f32) * scale) * scale
        gram = B["gf"][...]

        def mixing(gram, half):
            return (quintic_second * gram + quintic_third * dot(half, half)).astype(bf16)

        def advance(gram, half, mix):
            once = quintic_first * gram + dot(mix, half)
            return quintic_first * once + dot(once.astype(bf16), mix)

        B["gb"][...] = gram.astype(bf16)
        B["m0"][...] = mixing(gram, B["gb"][...])
        gram = advance(gram, B["gb"][...], B["m0"][...])
        B["gb"][...] = gram.astype(bf16)
        B["m1"][...] = mixing(gram, B["gb"][...])
        gram = advance(gram, B["gb"][...], B["m1"][...])
        B["gf"][...] = gram
        B["gb"][...] = gram.astype(bf16)
        mine = pl.ds(pl.multiple_of(x * 128, 128), 128)
        mix2 = (
            quintic_second * B["gf"][mine, :]
            + quintic_third * dot(B["gb"][mine, :], B["gb"][...])
        ).astype(bf16)
        k1 = quintic_first * (B["m1"][mine, :].astype(f32) + mix2.astype(f32)) + dot(
            mix2, B["m1"][...]
        )
        k0 = (
            quintic_first**2 * B["m0"][mine, :].astype(f32)
            + quintic_first * k1
            + dot(k1.astype(bf16), B["m0"][...])
        )
        last = quintic_first**3 * B["u"][x].astype(f32) + dot(
            k0.astype(bf16), B["u"][...].reshape(KV, 128)
        )
        last = (last * scale).astype(bf16)
        B["big"][c, y, x] = (factor * last.astype(f32)).astype(bf16)
    yield "ns", flush

    def sy(k):
        return remote("sy", B["big"].at[c, y, x], B["big"].at[c, y, x], ypeer(k), recv=y)

    def sx(m):
        for k in (2, 1, 3):
            remote("sx", B["big"].at[c, m, x], B["big"].at[c, m, x], xpeer(k), recv=m).start()

    @pl.when(worker)
    def _():
        sy(1).start()
        sy(7).start()
        sx(y)
        sy(2).start()
        sy(6).start()

    def drain_worker():
        sent("sy", B["yr"])
        for yy in range(NY):
            @pl.when(y != yy)
            def _(yy=yy):
                sq(yy).wait_send()

    for m in range(NM):
        not_mine(lambda m: received("ny", B["nm16"].at[m], recv=m), m)
    ns = remote("ns", B["nm16"].at[:, rows8(oc), :], B["nmsib"], sib)
    ns.start()
    pending.append(ns.wait_send)
    nm_out[:, :, cols(c)] = B["nm16"][:, rows8(c), :]
    ac.wait_recv()
    flush()
    ns.wait_recv()
    nm_out[:, :, cols(oc)] = B["nmsib"][...]

    def picks(m):
        mine = owners[m]
        slot = jnp.int32(0)
        for j in range(NM):
            slot = slot + ((owners[j] == mine) & (j < m)).astype(jnp.int32)
        return [(mine == d) & (slot == s) for s in range(MOST)]

    for m in range(NM):
        not_mine(lambda m: received("sq", B["sqr"].at[m], recv=m), m)
    lane = lax.broadcasted_iota(jnp.int32, (1, 128), 1)
    rms = jnp.zeros((1, 128), f32)
    for m in range(NM):
        value = jnp.sqrt(B["sqr"][m, 0:1, :] / float(KV * D))
        chosen = picks(m)
        for s in range(MOST):
            rms = rms + jnp.where(chosen[s] & (lane == s), value, 0.0)
    rms_out[...] = rms[:, 0:MOST]

    @pl.when(worker)
    def _():
        for k in (3, 5, 4):
            sy(k).start()

    def on_x(m, delta):
        received("sy", B["big"].at[c, m, x], recv=m)
        sx(m)

    each(NEAR[1:], on_x)
    pending.append(lambda: pl.when(worker)(drain_worker))
    pending.append(lambda: sent("sx", B["xr"]))
    yield "sy", flush

    def finish(cc, m):
        chosen = picks(m)

        def one(xx, carry):
            for yy in range(NY):
                rows = rows16(yy * 4 + xx)
                scaled = B["big"][cc, m, xx, pl.ds(yy * 16, 16), :]
                master = B["mb"][cc, xx, yy, m].astype(f32)
                w_out[m, rows, cols(cc)] = (
                    master * (1.0 - learn_rate * weight_decay) - learn_rate * scaled.astype(f32)
                ).astype(bf16)
                for s in range(MOST):
                    ow_out[s, rows, cols(cc)] = jnp.where(
                        chosen[s], scaled, ow_out[s, rows, cols(cc)]
                    )
            return carry

        lax.fori_loop(0, NX, one, 0)
        own = B["big"][cc, m, x, pl.ds(pl.multiple_of(y * 16, 16), 16), :].astype(f32)
        own = jnp.where(c == 0, own[0:8], own[8:16])
        ma_out[m, :, cols(cc)] = (
            B["mas"][m, :, cols(cc)] * (1.0 - learn_rate * weight_decay) - learn_rate * own
        )

    def to_sibling(m, delta):
        received("sx", B["big"].at[c, m, pl.ds(0, NX - 1)], recv=m)
        remote("sc", B["big"].at[c, m], B["big"].at[c, m], sib, recv=m).start()

    def from_sibling(m, delta):
        received("sc", B["big"].at[oc, m], recv=m)
        finish(oc, m)

    for i, delta in enumerate(NEAR):
        each((delta,), to_sibling)
        if i:
            each((NEAR[i - 1],), from_sibling)
        each((delta,), lambda m, delta: finish(c, m))
    each((NEAR[-1],), from_sibling)
    pending.append(lambda: sent("sc", B["big"].at[c]))
    flush()


def kernel(stop, *refs):
    for name, flush in stages(*refs):
        if name == stop:
            flush()
            break


def step(owners, g, mom, mas, stop=None, collective_id=0):
    vmem = pl.BlockSpec(memory_space=pltpu.VMEM)
    hbm = pl.BlockSpec(memory_space=pltpu.HBM)
    scratch = [pltpu.SMEM((NM,), jnp.int32)]
    scratch += [pltpu.VMEM(*spec) for spec in BUFFERS.values()]
    for send, recv in PHASES.values():
        scratch += [pltpu.SemaphoreType.DMA((send,)), pltpu.SemaphoreType.DMA((recv,))]
    return pl.pallas_call(
        functools.partial(kernel, stop),
        out_shape=(
            pltpu.VMEM((NM, KV, 256), bf16),
            pltpu.VMEM((NM, 8, 256), f32),
            pltpu.VMEM((NM, 8, 256), f32),
            pltpu.VMEM((MOST, KV, 256), bf16),
            pltpu.VMEM((1, MOST), f32),
        ),
        in_specs=[hbm, hbm, hbm, hbm],
        out_specs=(vmem, vmem, vmem, vmem, vmem),
        scratch_shapes=scratch,
        compiler_params=pltpu.CompilerParams(
            collective_id=collective_id, has_side_effects=True, vmem_limit_bytes=40 * 1024 * 1024
        ),
        name="muon_step",
    )(*(pltpu.with_memory_space_constraint(item, pltpu.HBM) for item in (owners, g, mom, mas)))


def copy_kernel(*refs):
    count = (len(refs) - 1) // 2
    copies = [
        pltpu.make_async_copy(refs[i], refs[count + i], refs[-1].at[i]) for i in range(count)
    ]
    for copy in copies:
        copy.start()
    for copy in copies:
        copy.wait()


def write_out(arrays):
    return pl.pallas_call(
        copy_kernel,
        out_shape=[jax.ShapeDtypeStruct(item.shape, item.dtype) for item in arrays],
        in_specs=[pl.BlockSpec(memory_space=pl.ANY)] * len(arrays),
        out_specs=[pl.BlockSpec(memory_space=pl.ANY)] * len(arrays),
        scratch_shapes=[pltpu.SemaphoreType.DMA((len(arrays),))],
        name="write_out",
    )(*(pltpu.with_memory_space_constraint(item, pltpu.VMEM) for item in arrays))


def per_device(gradients, momentum, master, owners):
    new_weights, new_momentum, new_master, owned_updates, owned_rms = write_out(
        step(owners, gradients[0], momentum, master)
    )
    return (new_weights, new_master, new_momentum, owned_updates[None], owned_rms)


def solution(mesh):
    return jax.shard_map(
        per_device,
        mesh=mesh,
        in_specs=(P("dp", None, None, "col"), P(None, "dp", "col"), P(None, "dp", "col"), P()),
        out_specs=(
            P(None, None, "col"),
            P(None, "dp", "col"),
            P(None, "dp", "col"),
            P("dp", None, None, "col"),
            P("dp", None),
        ),
        check_vma=False,
    )
```
